256 devices in a mesh: ctx: 16 (over x, z_lo), tp: 16 (over y, z_hi, core).
Axes of the slice: x: 4, y: 4, z: 8 (z_hi: 2, z_lo: 4; z = z_hi * 4 + z_lo), core: 2. Of those that a mesh axis runs over, the one named last changes fastest.
Arguments:
- layer_input: bfloat16 [4096, 7168], P('ctx', 'tp'), may hold values from -6 to 6
- q_latent: bfloat16 [4096, 1536], P('ctx'), may hold values from -384 to 384
- w_dkv: bfloat16 [7168, 576], P('tp'), may hold values from -0.0625 to 0.0625
- kv_gain: float32 [512], replicated, may hold values from 0.1 to 1.9
- w_uq: bfloat16 [1536, 12288], P(None, 'tp'), may hold values from -0.15625 to 0.15625
- w_uk: bfloat16 [64, 512, 128], P('tp'), may hold values from -1 to 1
- w_uv: bfloat16 [64, 512, 128], P('tp'), may hold values from -0.25 to 0.25
- w_o: bfloat16 [8192, 7168], P('tp'), may hold values from -0.09375 to 0.09375
- block_order: int32 [32], replicated, may hold values from 0 to 31, each once
- owner_slot: int32 [32], replicated, may hold values from 0 to 31, each once
Outputs:
- layer_out: bfloat16 [4096, 7168], P('ctx', 'tp')
- owner_cache: bfloat16 [4096, 576], P('ctx')
The draws below stay inside these ranges and needn't reach their ends.
Inputs may be any that keep to these rules, and one draw needn't show every extreme that they name: `block_order`: each of 0 to 31 once. `owner_slot`: each of 0 to 31 once.
All inputs are finite; a program needn't handle non-finite values.
Results may differ from the reference program's by a relative error of at most 0.02.
The reference program's roundings to bfloat16 on the way count: a program that leaves them out, or rounds other values in their place, can miss the bound.
Values may be sent and summed in bfloat16 or wider, within the bound.
A program may use at most 128 MiB of HBM per device.

```python
import math
import jax
import jax.numpy as jnp
from jax import lax

D = 7168
HEADS = 64
QLAT = 1536
LATENT = 512
NOPE = 128
VDIM = 128
QKD = 192
KVW = 576
HALF = 128
BLOCKS = 32
TOKENS = 4096
N_TP = 16


def draw_q_latent(key, part):
    key = jax.random.fold_in(key, 11)
    normal_draw = jnp.clip(jax.random.normal(key, (TOKENS, QLAT), jnp.float32), -6.0, 6.0)
    return normal_draw.astype(jnp.bfloat16)


def raised(entries, rng, source, target, parts, factor):
    def block_of(axis_at):
        return (jnp.arange(entries.shape[axis_at]) // (entries.shape[axis_at] // parts)).reshape((-1,) + (1,) * (entries.ndim - 1 - axis_at))

    near = jax.random.permutation(rng, parts)[block_of(target)]
    other_side = (block_of(target) + parts // 2) % parts
    return jnp.where((block_of(source) == near) | (block_of(source) == other_side), factor * entries, entries)


def steps_of(rng, dims, split, smallest, largest):
    level = 1.0
    for axis_at, parts in split:
        steps = jax.random.uniform(jax.random.fold_in(jax.random.fold_in(rng, 6), axis_at), (parts,), jnp.float32, smallest / len(split), largest / len(split))
        level = level * jnp.repeat(jnp.exp(steps), dims[axis_at] // parts).reshape((-1,) + (1,) * (len(dims) - 1 - axis_at))
    return level


def scatter_about(key, shape, deviation, most, pieces=(), kind=jnp.bfloat16):
    entries = deviation * jax.random.normal(key, shape, jnp.float32)
    if pieces:
        entries = entries * steps_of(key, shape, pieces, -0.22, 0.18)
    return jnp.clip(entries, -most, most).astype(kind)


def bell_draw_with(own_key, extent, scale, limit, pieces, heavy, held_as=jnp.bfloat16):
    drawn = scale * jax.random.normal(own_key, extent, jnp.float32)
    if pieces:
        drawn = drawn * steps_of(own_key, extent, pieces, -0.22, 0.18)
    return jnp.clip(raised(drawn, jax.random.fold_in(own_key, 3), *heavy), -limit, limit).astype(held_as)


def setup_inputs(seed: int = 0) -> dict:
    arg_keys = jax.random.split(jax.random.key(seed), 11)
    return {
        "layer_input": scatter_about(arg_keys[0], (TOKENS, D), 1.0, 6.0, ((0, 16), (1, 16))),
        "q_latent": draw_q_latent(jax.random.fold_in(arg_keys[10], 71), 0),
        "w_dkv": scatter_about(arg_keys[2], (D, KVW), D ** -0.5, 0.0625, ((0, 16),)),
        "kv_gain": jnp.clip(1.0 + 0.18 * jax.random.normal(arg_keys[3], (LATENT,), jnp.float32), 0.1, 1.9),
        "w_uq": scatter_about(arg_keys[4], (QLAT, HEADS * QKD), QLAT ** -0.5, 0.15625, ((1, 16),)),
        "w_uk": scatter_about(arg_keys[5], (HEADS, LATENT, NOPE), (NOPE // 4) ** -0.5, 1.0, ((0, 16),)),
        "w_uv": scatter_about(arg_keys[6], (HEADS, LATENT, VDIM), LATENT ** -0.5, 0.25, ((0, 16),)),
        "w_o": bell_draw_with(arg_keys[7], (HEADS * VDIM, D), (HEADS * VDIM) ** -0.5, 0.09375, ((0, 16),), (0, 1, 16, 2.0)),
        "block_order": jax.random.permutation(arg_keys[8], BLOCKS).astype(jnp.int32),
        "owner_slot": jax.random.permutation(arg_keys[9], BLOCKS).astype(jnp.int32),
    }


def rotate(values_in, places):
    width = values_in.shape[-1]
    half_w = width // 2
    frequency = jnp.exp(jnp.arange(half_w).astype(jnp.float32) * (-2.0 * math.log(10000.0) / width))
    angles = places.astype(jnp.float32)[:, None] * frequency[None, :]
    cosine = jnp.cos(angles)
    sines = jnp.sin(angles)
    front_part = values_in[..., :half_w]
    back_part = values_in[..., half_w:]
    return jnp.concatenate([front_part * cosine - back_part * sines, front_part * sines + back_part * cosine], -1)

def finish_rows(kv_rows, places, kv_gain, latent):
    compressed = kv_rows[:, :latent]
    mean_square = lax.optimization_barrier(jnp.mean(compressed * compressed, axis=1, keepdims=True))
    compressed = compressed * lax.rsqrt(mean_square + 1e-06) * kv_gain
    return jnp.concatenate([compressed, rotate(kv_rows[:, latent:], places)], 1).astype(jnp.bfloat16)

def reference(layer_input, q_latent, w_dkv, kv_gain, w_uq, w_uk, w_uv, w_o, block_order, owner_slot):
    all_rows = jnp.arange(TOKENS, dtype=jnp.int32)
    places = (block_order[all_rows // HALF] * HALF + all_rows % HALF).astype(jnp.int32)
    inverse_order = jnp.zeros((BLOCKS,), jnp.int32).at[block_order].set(jnp.arange(BLOCKS, dtype=jnp.int32))
    from_prompt = (inverse_order[all_rows // HALF] * HALF + all_rows % HALF).astype(jnp.int32)
    kv_full = jnp.dot(layer_input, w_dkv, preferred_element_type=jnp.float32)
    cache = finish_rows(kv_full, places, kv_gain, LATENT)
    prompt_cache = cache[from_prompt]
    prompt_latent = q_latent[from_prompt]
    head_weights = w_uq.reshape(QLAT, HEADS, QKD).transpose(1, 0, 2)
    block_rows = TOKENS // 8
    score_scale = QKD ** (-0.5)

    def one_head(operands):
        w_query, w_key, w_value = operands
        q_proj = jnp.dot(prompt_latent, w_query, preferred_element_type=jnp.float32)
        q_nope = q_proj[:, :NOPE].astype(jnp.bfloat16)
        q_absorbed = jnp.dot(q_nope, w_key.T, preferred_element_type=jnp.float32).astype(jnp.bfloat16)
        q_rotary = rotate(q_proj[:, NOPE:], all_rows).astype(jnp.bfloat16)
        queries = jnp.concatenate([q_absorbed, q_rotary], 1)
        outputs = []
        for block_index in range(8):
            lower = block_index * block_rows
            upper = lower + block_rows
            q_block = queries[lower:upper]
            keys_here = prompt_cache[:upper]
            scores = jnp.dot(q_block, keys_here.T, preferred_element_type=jnp.float32) * score_scale
            visible = all_rows[:upper][None, :] <= all_rows[lower:upper][:, None]
            scores = jnp.where(visible, scores, -1e+30)
            peak = lax.optimization_barrier(jnp.max(scores, axis=1, keepdims=True))
            weights = jnp.where(visible, jnp.exp(scores - peak), 0.0)
            totals = lax.optimization_barrier(jnp.sum(weights, axis=1, keepdims=True))
            context = (jnp.dot(weights.astype(jnp.bfloat16), keys_here[:, :LATENT], preferred_element_type=jnp.float32) / totals).astype(jnp.bfloat16)
            outputs.append(jnp.dot(context, w_value, preferred_element_type=jnp.float32).astype(jnp.bfloat16))
        return jnp.concatenate(outputs, 0)
    head_out = lax.map(one_head, (head_weights, w_uk, w_uv))
    device_values = head_out[:, places, :].transpose(1, 0, 2).reshape(TOKENS, HEADS * VDIM)
    group_width = HEADS * VDIM // N_TP

    def add_group(total_sum, group_index):
        values_part = lax.dynamic_slice_in_dim(device_values, group_index * group_width, group_width, 1)
        weights_part = lax.dynamic_slice_in_dim(w_o, group_index * group_width, group_width, 0)
        term = jnp.dot(values_part, weights_part, preferred_element_type=jnp.float32).astype(jnp.bfloat16)
        term = lax.optimization_barrier(term)
        return (total_sum + term.astype(jnp.float32), None)
    layer_sum, _ = lax.scan(add_group, jnp.zeros((TOKENS, D), jnp.float32), jnp.arange(N_TP, dtype=jnp.int32))
    inverse_owner = jnp.zeros((BLOCKS,), jnp.int32).at[owner_slot].set(jnp.arange(BLOCKS, dtype=jnp.int32))
    owner_rows = (inverse_owner[all_rows // HALF] * HALF + all_rows % HALF).astype(jnp.int32)
    owner_cache = prompt_cache[owner_rows]
    return (layer_sum.astype(jnp.bfloat16), owner_cache)
```

```python
import functools
import math

import jax
import jax.numpy as jnp
from jax import lax
from jax.experimental import pallas as pl
from jax.experimental.pallas import tpu as pltpu
from jax.sharding import PartitionSpec as P

MESH = pl.DeviceIdType.MESH
F32 = jnp.float32
BF16 = jnp.bfloat16
ROWS = 256
HALF = 128
LAT = 512
ROPE = 64
KVW = 576
NOPE = 128
HEADS = 4
MODEL = 7168
BLK = 896
SCALE = 192.0 ** -0.5 * math.log2(math.e)


def dot(a, b):
    return jnp.dot(a, b, preferred_element_type=F32)


def dot_t(a, b):
    return lax.dot_general(a, b, (((1,), (1,)), ((), ())), preferred_element_type=F32)


def rope(v, cos, sin):
    a, b = v[:, :32], v[:, 32:64]
    return jnp.concatenate([a * cos - b * sin, a * sin + b * cos], 1)


def kernel(
    li_hbm, ql_hbm, wdkv_hbm, gain_ref, wuq_hbm, wuk_hbm, wuv_hbm, wo_hbm, order_ref, order_row, slot_row,
    out_ref, own_ref,
    li, ql, wdkv, wuq, wuk, wuv, wo, wo2,
    part, part_recv, ysum, yrecv, zsend, zrecv,
    cos_ref, sin_ref, queries, cache, m_ref, l_ref, acc,
    hv, hv_recv, far_send, far_recv, near_send, near_recv, zo_send, zo_recv, fin, fin_recv,
    ld_sem, wo_ssem, wo_rsem, p_sem, y_sem, z_sem, p1_sem, p2_sem, p3_sem, sh_sem,
    hv_sem, far_sem, near_sem, zo_sem, fin_sem,
):
    c_idx = lax.axis_index("ctx")
    t_idx = lax.axis_index("tp")
    x, zl = c_idx // 4, c_idx % 4
    y, zh, k = t_idx // 4, (t_idx // 2) % 2, t_idx % 2
    z = zh * 4 + zl
    j = 1 - k

    def device(dx=0, dy=0, dz=0, dk=0):
        nx, ny, nz, nk = (x + dx + 4) % 4, (y + dy + 4) % 4, (z + dz + 8) % 8, (k + dk) % 2
        return (nx * 4 + nz % 4, ny * 4 + (nz // 4) * 2 + nk)

    sibling = device(dk=1)

    def remote(src, dst, sem, where):
        copy = pltpu.make_async_remote_copy(
            src_ref=src, dst_ref=dst, send_sem=sem.at[0], recv_sem=sem.at[1],
            device_id=where, device_id_type=MESH,
        )
        return copy

    loads = []
    for i, (src, dst) in enumerate(
        ((li_hbm, li), (wdkv_hbm, wdkv), (ql_hbm, ql), (wuq_hbm, wuq), (wuk_hbm, wuk), (wuv_hbm, wuv), (wo_hbm, wo))
    ):
        loads.append(pltpu.make_async_copy(src, dst, ld_sem.at[i]))
    for copy in loads[:6]:
        copy.start()

    barrier = pltpu.get_barrier_semaphore()
    peers = [
        sibling, device(dy=1), device(dy=-1), device(dy=2), device(dz=4),
        device(dx=1), device(dx=-1), device(dx=2),
        device(dz=1), device(dz=-1), device(dz=2), device(dz=-2),
    ]
    for peer in peers:
        pl.semaphore_signal(barrier, inc=1, device_id=peer, device_id_type=MESH)

    row_id = lax.broadcasted_iota(jnp.int32, (ROWS, 1), 0)
    first, second = order_ref[2 * c_idx] * HALF, order_ref[2 * c_idx + 1] * HALF
    places = jnp.where(row_id < HALF, first + row_id, second + row_id - HALF)

    loads[0].wait()
    loads[1].wait()
    part[pl.ds(j * HALF, HALF), :] = dot(li[pl.ds(pl.multiple_of(j * HALF, HALF), HALF), :], wdkv[...])
    part[pl.ds(k * HALF, HALF), :] = dot(li[pl.ds(pl.multiple_of(k * HALF, HALF), HALF), :], wdkv[...])
    pl.semaphore_wait(barrier, len(peers))
    cp = remote(part.at[pl.ds(pl.multiple_of(j * HALF, HALF), HALF)], part_recv, p_sem, sibling)
    cp.start()

    frequency = jnp.exp(
        lax.broadcasted_iota(jnp.int32, (1, 32), 1).astype(F32) * (-2.0 * math.log(10000.0) / ROPE)
    )
    angles = places.astype(F32) * frequency
    cos_ref[...] = jnp.cos(angles)
    sin_ref[...] = jnp.sin(angles)

    cp.wait()
    ysum[...] = part[pl.ds(pl.multiple_of(k * HALF, HALF), HALF), :] + part_recv[...]
    copies = []
    for i, d in enumerate((1, -1, 2)):
        ny = (y + d + 4) % 4
        cp = remote(
            ysum.at[pl.ds(pl.multiple_of(ny * 32, 32), 32)], yrecv.at[i], y_sem.at[i], device(dy=d)
        )
        cp.start()
        copies.append(cp)
    wo_far = pltpu.make_async_remote_copy(
        src_ref=wo_hbm, dst_ref=wo2, send_sem=wo_ssem, recv_sem=wo_rsem, device_id=sibling, device_id_type=MESH
    )
    wo_far.start()
    loads[6].start()

    loads[2].wait()
    loads[3].wait()
    q_proj = dot(ql[...], wuq[...])
    loads[4].wait()

    def absorb(h):
        q_nope = q_proj[:, 192 * h : 192 * h + NOPE].astype(BF16)
        queries[h, :, :LAT] = dot_t(q_nope, wuk[h]).astype(BF16)
        queries[h, :, LAT:] = rope(
            q_proj[:, 192 * h + NOPE : 192 * h + 192], cos_ref[...], sin_ref[...]
        ).astype(BF16)

    absorb(0)
    absorb(1)
    for cp in copies:
        cp.wait()
    zsend[...] = ((ysum[pl.ds(pl.multiple_of(y * 32, 32), 32), :] + yrecv[0]) + yrecv[1]) + yrecv[2]
    cp = remote(zsend, zrecv, z_sem, device(dz=4))
    cp.start()
    absorb(2)
    absorb(3)
    cp.wait()
    kv = zsend[...] + zrecv[...]
    latent = kv[:, :LAT]
    mean_square = jnp.mean(latent * latent, axis=1, keepdims=True)
    latent = latent * lax.rsqrt(mean_square + 1e-6) * gain_ref[...]
    own_row = pl.multiple_of(k * HALF + y * 32, 32)
    rotated = rope(kv[:, LAT:], cos_ref[pl.ds(own_row, 32), :], sin_ref[pl.ds(own_row, 32), :])

    a_own = x * j + zl * k
    b_own = zl * j + y * k
    c_own = y * j + x * k
    b_sib = zl * k + y * j
    c_sib = y * k + x * j

    def at(core, b, c, a=0, extra=0):
        return pl.multiple_of(core * 2048 + b * 512 + c * 128 + a * 32 + extra, 32)

    own_at = at(k, b_own, c_own, a_own)
    cache[pl.ds(own_at, 32), :] = jnp.concatenate([latent, rotated], 1).astype(BF16)
    own_slab = cache.at[pl.ds(own_at, 32)]
    copies = []
    for i, d in enumerate((1, -1, 2)):
        cp = remote(own_slab, own_slab, p1_sem.at[i], device(dx=d * j, dz=d * k))
        cp.start()
        copies.append(cp)
    for cp in copies:
        cp.wait()

    def group(b, c):
        return cache.at[pl.ds(at(k, b, c), 128)]

    pending = []

    def send_group(r, b):
        mine = group(b, c_own)
        for i, d in enumerate((1, -1, 2)):
            cp = remote(mine, mine, p3_sem.at[r, i], device(dy=d * j, dx=d * k))
            cp.start()
            pending.append(cp)
        cp = remote(mine, mine, sh_sem.at[r, 3], sibling)
        cp.start()
        pending.append(cp)

    mine = group(b_own, c_own)
    half_a = cache.at[pl.ds(at(k, b_own, c_own), 64)]
    half_b = cache.at[pl.ds(at(k, b_own, c_own, 0, 64), 64)]
    second_phase = []
    for i, (src, d) in enumerate(((mine, 1), (mine, -1), (half_a, 2), (half_b, -2))):
        cp = remote(src, src, p2_sem.at[i], device(dz=d * j, dy=d * k))
        cp.start()
        second_phase.append(cp)
    order = [0, 3, 1, 2]
    send_group(0, b_own)
    second_phase[0].wait()
    send_group(1, (b_own + 3) % 4)
    second_phase[1].wait()
    send_group(2, (b_own + 1) % 4)
    second_phase[2].wait()
    second_phase[3].wait()
    send_group(3, (b_own + 2) % 4)

    lane = lax.broadcasted_iota(jnp.int32, (1, 128), 1)

    def bias_of(core, b):
        other = 1 - core
        pieces = []
        for c in range(4):
            held = []
            for a in range(4):
                ctx = (4 * a + b) * other + (4 * c + a) * core
                held.append(order_ref[2 * ctx + core] * HALF)
            base = jnp.where(
                lane < 64, jnp.where(lane < 32, held[0], held[1]), jnp.where(lane < 96, held[2], held[3])
            )
            pieces.append(base + lane % 32 + 32 * (c * other + b * core))
        key_places = jnp.concatenate(pieces, 1)
        return jnp.where(key_places <= places, 0.0, -1e30)

    m_ref[...] = jnp.full(m_ref.shape, -1e29, F32)
    l_ref[...] = jnp.zeros(l_ref.shape, F32)
    acc[...] = jnp.zeros(acc.shape, F32)

    def attend(core, b):
        bias = bias_of(core, b)
        rows = pl.ds(at(core, b, 0), 512)

        def heads(i, carry):
            for u in range(2):
                h = 2 * i + u
                scores = dot_t(queries[h], cache[rows, :]) * SCALE + bias
                m_old = m_ref[h]
                m_new = jnp.maximum(m_old, jnp.max(scores, axis=1, keepdims=True))
                alpha = jnp.exp2(m_old - m_new)
                probs = jnp.exp2(scores - m_new[:, :1])
                l_ref[h] = l_ref[h] * alpha + jnp.sum(probs, axis=1, keepdims=True)
                m_ref[h] = m_new
                acc[h] = acc[h] * alpha[:, :1] + dot(probs.astype(BF16), cache[rows, :LAT])
            return carry

        lax.fori_loop(0, 2, heads, 0)

    for r in range(4):
        b = (b_own + order[r]) % 4
        for i, d in enumerate((1, -1, 2)):
            remote(mine, mine, p3_sem.at[r, i], sibling).wait_recv()
            got = group(b, (c_own - d + 4) % 4)
            cp = remote(got, got, sh_sem.at[r, i], sibling)
            cp.start()
            pending.append(cp)
        attend(k, b)
        for i in range(4):
            remote(mine, mine, sh_sem.at[r, i], sibling).wait_recv()
        attend(j, (b_sib + order[r]) % 4)

    loads[5].wait()
    for h in range(HEADS):
        context = (acc[h] / l_ref[h][:, :1]).astype(BF16)
        hv[:, 128 * h : 128 * (h + 1)] = dot(context, wuv[h]).astype(BF16)
    hv_copy = remote(hv.at[pl.ds(pl.multiple_of(j * HALF, HALF), HALF)], hv_recv, hv_sem, sibling)
    hv_copy.start()

    number = lax.broadcasted_iota(jnp.int32, (1, 32), 1)
    sources = []
    for i in range(2):
        prompt = jnp.sum(jnp.where(slot_row[...] == 2 * c_idx + i, number, 0), axis=1, keepdims=True)
        held = jnp.sum(jnp.where(order_row[...] == prompt, number, 0), axis=1, keepdims=True)
        core, hx, hz = held & 1, held >> 3, (held >> 1) & 3
        row = row_id[:HALF]
        q, rest = row >> 5, row & 31
        zero = hz * 512 + q * 128 + hx * 32 + rest
        one = 2048 + q * 512 + hx * 128 + hz * 32 + rest
        sources.append(jnp.where(core == 0, zero, one))
    source = jnp.concatenate(sources, 0)
    key_lane = lax.broadcasted_iota(jnp.int32, (1, 1024), 1)
    picked_rows = jnp.zeros((ROWS, KVW), F32)
    for n in range(4):
        picked = jnp.where(key_lane + 1024 * n == source, 1.0, 0.0).astype(BF16)
        picked_rows = picked_rows + dot(picked, cache[1024 * n : 1024 * (n + 1), :])
    own_ref[...] = picked_rows.astype(BF16)

    loads[6].wait()
    wo_far.wait()
    hv_copy.wait()
    hv_own_rows = pl.ds(pl.multiple_of(k * HALF, HALF), HALF)

    def partial(dy, zz):
        columns = pl.ds(pl.multiple_of((((y + dy + 4) % 4) * 2 + zz) * BLK, 128), BLK)
        return dot(hv[hv_own_rows, :], wo[:, columns]) + dot(hv_recv[...], wo2[:, columns])

    up, down = device(dy=1), device(dy=-1)
    near = {}
    sides = ((0, 1 - zh), (1, zh))
    far = {}
    for s, zz in sides:
        p = partial(2, zz).astype(BF16)
        for i, where in enumerate((up, down)):
            far_send[s, i] = p[64 * i : 64 * (i + 1)]
            cp = remote(far_send.at[s, i], far_recv.at[s, i], far_sem.at[s, i], where)
            cp.start()
            far[s, i] = cp
        for e, (dy, where) in enumerate(((1, up), (-1, down))):
            p = partial(dy, zz)
            near_send[s, e, 1 - e] = p[64 * (1 - e) : 64 * (2 - e)].astype(BF16)
            cp = remote(near_send.at[s, e, 1 - e], near_recv.at[s, e, 1 - e], near_sem.at[s, e, 1 - e], where)
            cp.start()
            near[s, e, 1 - e] = cp
            far[s, e].wait()
            near_send[s, e, e] = (p[64 * e : 64 * (e + 1)] + far_recv[s, e].astype(F32)).astype(BF16)
            cp = remote(near_send.at[s, e, e], near_recv.at[s, e, e], near_sem.at[s, e, e], where)
            cp.start()
            near[s, e, e] = cp
    for s, zz in sides:
        p = partial(0, zz)
        for e in range(2):
            for f in range(2):
                near[s, e, f].wait()
        total = p + (
            jnp.concatenate([near_recv[s, 0, 0], near_recv[s, 0, 1]], 0).astype(F32)
            + jnp.concatenate([near_recv[s, 1, 0], near_recv[s, 1, 1]], 0).astype(F32)
        )
        if s == 0:
            zo_send[...] = total.astype(BF16)
            zo_copy = remote(zo_send, zo_recv, zo_sem, device(dz=4))
            zo_copy.start()
    zo_copy.wait()
    fin[...] = (total + zo_recv[...].astype(F32)).astype(BF16)
    fin_copy = remote(fin, fin_recv, fin_sem, sibling)
    fin_copy.start()
    mine_here = fin[...]
    out_ref[hv_own_rows, :] = jnp.where(k == 0, mine_here[:, :448], mine_here[:, 448:])
    fin_copy.wait()
    theirs = fin_recv[...]
    out_ref[pl.ds(pl.multiple_of(j * HALF, HALF), HALF), :] = jnp.where(k == 0, theirs[:, :448], theirs[:, 448:])
    for cp in pending:
        cp.wait_send()


def per_device(
    layer_input, q_latent, w_dkv, kv_gain, w_uq, w_uk, w_uv, w_o, block_order, owner_slot
):
    hbm = pl.BlockSpec(memory_space=pl.ANY)
    vmem = pl.BlockSpec(memory_space=pltpu.VMEM)
    smem = pl.BlockSpec(memory_space=pltpu.SMEM)
    V = pltpu.VMEM
    dma = pltpu.SemaphoreType.DMA
    return pl.pallas_call(
        kernel,
        out_shape=(
            jax.ShapeDtypeStruct((ROWS, 448), BF16),
            jax.ShapeDtypeStruct((ROWS, KVW), BF16),
        ),
        in_specs=[hbm, hbm, hbm, vmem, hbm, hbm, hbm, hbm, smem, vmem, vmem],
        out_specs=(vmem, vmem),
        scratch_shapes=[
            V((ROWS, 448), BF16), V((ROWS, 1536), BF16), V((448, KVW), BF16), V((1536, 768), BF16),
            V((HEADS, LAT, NOPE), BF16), V((HEADS, LAT, NOPE), BF16), V((512, MODEL), BF16), V((512, MODEL), BF16),
            V((ROWS, KVW), F32), V((HALF, KVW), F32), V((HALF, KVW), F32), V((3, 32, KVW), F32),
            V((32, KVW), F32), V((32, KVW), F32),
            V((ROWS, 32), F32), V((ROWS, 32), F32), V((HEADS, ROWS, KVW), BF16), V((4096, KVW), BF16),
            V((HEADS, ROWS, 128), F32), V((HEADS, ROWS, 128), F32), V((HEADS, ROWS, LAT), F32),
            V((ROWS, 512), BF16), V((HALF, 512), BF16),
            V((2, 2, 64, BLK), BF16), V((2, 2, 64, BLK), BF16),
            V((2, 2, 2, 64, BLK), BF16), V((2, 2, 2, 64, BLK), BF16),
            V((HALF, BLK), BF16), V((HALF, BLK), BF16), V((HALF, BLK), BF16), V((HALF, BLK), BF16),
            dma((7,)), dma, dma, dma((2,)), dma((3, 2)), dma((2,)), dma((3, 2)), dma((4, 2)),
            dma((4, 3, 2)), dma((4, 4, 2)), dma((2,)), dma((2, 2, 2)), dma((2, 2, 2, 2)), dma((2,)), dma((2,)),
        ],
        compiler_params=pltpu.CompilerParams(
            collective_id=0, has_side_effects=True, vmem_limit_bytes=60 * 1024 * 1024
        ),
    )(
        layer_input, q_latent, w_dkv, kv_gain.reshape(1, LAT), w_uq, w_uk, w_uv, w_o,
        block_order, block_order.reshape(1, 32), owner_slot.reshape(1, 32),
    )


def solution(mesh):
    return jax.shard_map(
        per_device,
        mesh=mesh,
        in_specs=(
            P("ctx", "tp"),
            P("ctx", None),
            P("tp", None),
            P(),
            P(None, "tp"),
            P("tp", None, None),
            P("tp", None, None),
            P("tp", None),
            P(),
            P(),
        ),
        out_specs=(P("ctx", "tp"), P("ctx", None)),
        check_vma=False,
    )
```

```python
import functools
import math

import jax
import jax.numpy as jnp
from jax import lax
from jax.experimental import pallas as pl
from jax.experimental.pallas import tpu as pltpu
from jax.sharding import PartitionSpec as P

MESH = pl.DeviceIdType.MESH
F32 = jnp.float32
BF16 = jnp.bfloat16
ROWS = 256
HALF = 128
LAT = 512
ROPE = 64
KVW = 576
NOPE = 128
HEADS = 4
MODEL = 7168
BLK = 896
SCALE = 192.0 ** -0.5 * math.log2(math.e)


def dot(a, b):
    return jnp.dot(a, b, preferred_element_type=F32)


def dot_t(a, b):
    return lax.dot_general(a, b, (((1,), (1,)), ((), ())), preferred_element_type=F32)


def rope(v, cos, sin):
    a, b = v[:, :32], v[:, 32:64]
    return jnp.concatenate([a * cos - b * sin, a * sin + b * cos], 1)


def kernel(
    li_hbm, ql_hbm, wdkv_hbm, gain_ref, wuq_hbm, wuk_hbm, wuv_hbm, wo_hbm, order_ref, order_row, slot_row,
    out_ref, own_ref,
    li, ql, wdkv, wuq, wuk, wuv, wo, wo2,
    part, part_recv, ysum, yrecv, zsend, zrecv,
    cos_ref, sin_ref, queries, cache, m_ref, l_ref, acc,
    hv, hv_recv, far_send, far_recv, near_send, near_recv, zo_send, zo_recv, fin, fin_recv,
    ld_sem, wo_ssem, wo_rsem, p_sem, y_sem, z_sem, p1_sem, p2_sem, p3_sem, p4_sem, sh_sem,
    hv_sem, far_sem, near_sem, zo_sem, fin_sem,
):
    c_idx = lax.axis_index("ctx")
    t_idx = lax.axis_index("tp")
    x, zl = c_idx // 4, c_idx % 4
    y, zh, k = t_idx // 4, (t_idx // 2) % 2, t_idx % 2
    z = zh * 4 + zl
    j = 1 - k

    def device(dx=0, dy=0, dz=0, dk=0):
        nx, ny, nz, nk = (x + dx + 4) % 4, (y + dy + 4) % 4, (z + dz + 8) % 8, (k + dk) % 2
        return (nx * 4 + nz % 4, ny * 4 + (nz // 4) * 2 + nk)

    sibling = device(dk=1)

    def remote(src, dst, sem, where):
        copy = pltpu.make_async_remote_copy(
            src_ref=src, dst_ref=dst, send_sem=sem.at[0], recv_sem=sem.at[1],
            device_id=where, device_id_type=MESH,
        )
        return copy

    loads = []
    for i, (src, dst) in enumerate(
        ((li_hbm, li), (wdkv_hbm, wdkv), (ql_hbm, ql), (wuq_hbm, wuq), (wuk_hbm, wuk), (wuv_hbm, wuv), (wo_hbm, wo))
    ):
        loads.append(pltpu.make_async_copy(src, dst, ld_sem.at[i]))
    for copy in loads[:6]:
        copy.start()

    barrier = pltpu.get_barrier_semaphore()
    peers = [
        sibling, device(dy=1), device(dy=-1), device(dy=2), device(dz=4),
        device(dx=1), device(dx=-1), device(dx=2),
        device(dz=1), device(dz=-1), device(dz=2), device(dz=-2),
    ]
    for peer in peers:
        pl.semaphore_signal(barrier, inc=1, device_id=peer, device_id_type=MESH)

    row_id = lax.broadcasted_iota(jnp.int32, (ROWS, 1), 0)
    first, second = order_ref[2 * c_idx] * HALF, order_ref[2 * c_idx + 1] * HALF
    places = jnp.where(row_id < HALF, first + row_id, second + row_id - HALF)

    loads[0].wait()
    loads[1].wait()
    part[...] = lax.dot_general(li[...], wdkv[...], (((0,), (0,)), ((), ())), preferred_element_type=F32)
    pl.semaphore_wait(barrier, len(peers))
    cp = remote(part.at[pl.ds(pl.multiple_of(j * HALF, HALF), HALF)], part_recv, p_sem, sibling)
    cp.start()

    frequency = jnp.exp(
        lax.broadcasted_iota(jnp.int32, (1, 32), 1).astype(F32) * (-2.0 * math.log(10000.0) / ROPE)
    )
    angles = places.astype(F32) * frequency
    cos_ref[...] = jnp.cos(angles)
    sin_ref[...] = jnp.sin(angles)

    cp.wait()
    ysum[...] = part[pl.ds(pl.multiple_of(k * HALF, HALF), HALF), :] + part_recv[...]
    copies = []
    for i, d in enumerate((1, -1, 2)):
        ny = (y + d + 4) % 4
        cp = remote(
            ysum.at[pl.ds(pl.multiple_of(ny * 32, 32), 32)], yrecv.at[i], y_sem.at[i], device(dy=d)
        )
        cp.start()
        copies.append(cp)
    wo_far = pltpu.make_async_remote_copy(
        src_ref=wo_hbm, dst_ref=wo2, send_sem=wo_ssem, recv_sem=wo_rsem, device_id=sibling, device_id_type=MESH
    )
    wo_far.start()
    loads[6].start()

    loads[2].wait()
    loads[3].wait()
    q_proj = dot(ql[...], wuq[...])
    loads[4].wait()

    def absorb(h):
        q_nope = q_proj[:, 192 * h : 192 * h + NOPE].astype(BF16)
        queries[h, :, :LAT] = dot_t(q_nope, wuk[h]).astype(BF16)
        queries[h, :, LAT:] = rope(
            q_proj[:, 192 * h + NOPE : 192 * h + 192], cos_ref[...], sin_ref[...]
        ).astype(BF16)

    absorb(0)
    absorb(1)
    for cp in copies:
        cp.wait()
    zsend[...] = ((ysum[pl.ds(pl.multiple_of(y * 32, 32), 32), :] + yrecv[0]) + yrecv[1]) + yrecv[2]
    cp = remote(zsend, zrecv, z_sem, device(dz=4))
    cp.start()
    absorb(2)
    absorb(3)
    cp.wait()
    kv = zsend[...] + zrecv[...]
    latent = kv[:, :LAT]
    mean_square = jnp.mean(latent * latent, axis=1, keepdims=True)
    latent = latent * lax.rsqrt(mean_square + 1e-6) * gain_ref[...]
    own_row = pl.multiple_of(k * HALF + y * 32, 32)
    rotated = rope(kv[:, LAT:], cos_ref[pl.ds(own_row, 32), :], sin_ref[pl.ds(own_row, 32), :])

    a_own = x * j + y * k
    c_own = y * j + x * k

    def at(core, b, c, a=0, extra=0):
        return pl.multiple_of(core * 2048 + b * 512 + c * 128 + a * 32 + extra, 32)

    own_at = at(k, zl, c_own, a_own)
    cache[pl.ds(own_at, 32), :] = jnp.concatenate([latent, rotated], 1).astype(BF16)
    own_slab = cache.at[pl.ds(own_at, 32)]
    copies = []
    for i, d in enumerate((1, -1, 2)):
        cp = remote(own_slab, own_slab, p1_sem.at[i], device(dx=d * j, dy=d * k))
        cp.start()
        copies.append(cp)
    for cp in copies:
        cp.wait()

    def group(b, c):
        return cache.at[pl.ds(at(k, b, c), 128)]

    def half(b, c, e):
        return cache.at[pl.ds(at(k, b, c, 0, 64 * e), 64)]

    c_up, c_down = device(dy=j, dx=k), device(dy=-j, dx=-k)
    mine = group(zl, c_own)
    mine_half = half(zl, c_own, 0)

    def share(r, i, src):
        remote(src, src, sh_sem.at[r, i], sibling).start()

    def send_group(r, b):
        src = group(b, c_own)
        remote(src, src, p3_sem.at[r, 0], c_up).start()
        remote(src, src, p3_sem.at[r, 1], c_down).start()
        share(r, 3, src)

    def near_groups(r, b):
        below, above = (c_own + 3) % 4, (c_own + 1) % 4
        remote(mine, mine, p3_sem.at[r, 0], sibling).wait_recv()
        src = half(b, below, 0)
        remote(src, src, p4_sem.at[r, 0], c_up).start()
        share(r, 0, group(b, below))
        remote(mine, mine, p3_sem.at[r, 1], sibling).wait_recv()
        src = half(b, above, 1)
        remote(src, src, p4_sem.at[r, 1], c_down).start()
        share(r, 1, group(b, above))

    def far_group(r, b):
        for e in range(2):
            remote(mine_half, mine_half, p4_sem.at[r, e], sibling).wait_recv()
        share(r, 2, group(b, (c_own + 2) % 4))

    def shared(r):
        for i in range(4):
            remote(mine, mine, sh_sem.at[r, i], sibling).wait_recv()

    second_phase = []
    for i, (src, d) in enumerate(((mine, 1), (mine, -1), (half(zl, c_own, 0), 2), (half(zl, c_own, 1), -2))):
        cp = remote(src, src, p2_sem.at[i], device(dz=d))
        cp.start()
        second_phase.append(cp)

    lane = lax.broadcasted_iota(jnp.int32, (1, 128), 1)

    def bias_of(core, b):
        other = 1 - core
        pieces = []
        for c in range(4):
            held = []
            for a in range(4):
                ctx = 4 * (a * other + c * core) + b
                held.append(order_ref[2 * ctx + core] * HALF)
            base = jnp.where(
                lane < 64, jnp.where(lane < 32, held[0], held[1]), jnp.where(lane < 96, held[2], held[3])
            )
            pieces.append(base + lane % 32 + 32 * c * other + (lane // 32) * 32 * core)
        key_places = jnp.concatenate(pieces, 1)
        return jnp.where(key_places <= places, 0.0, -1e30)

    m_ref[...] = jnp.full(m_ref.shape, -1e29, F32)
    l_ref[...] = jnp.zeros(l_ref.shape, F32)
    acc[...] = jnp.zeros(acc.shape, F32)

    def attend(core, b):
        bias = bias_of(core, b)
        rows = pl.ds(at(core, b, 0), 512)

        def add_product(h, alpha, probs):
            acc[h] = acc[h] * alpha + dot(probs, cache[rows, :LAT])

        scores_next = dot_t(queries[0], cache[rows, :])
        last = None
        for h in range(HEADS):
            scores = scores_next
            if h + 1 < HEADS:
                scores_next = dot_t(queries[h + 1], cache[rows, :])
            if last is not None:
                add_product(*last)
            scores = scores * SCALE + bias
            m_old = m_ref[h]
            m_new = jnp.maximum(m_old, jnp.max(scores, axis=1, keepdims=True))
            alpha = jnp.exp2(m_old - m_new)
            probs = jnp.exp2(scores - m_new[:, :1])
            l_ref[h] = l_ref[h] * alpha + jnp.sum(probs, axis=1, keepdims=True)
            m_ref[h] = m_new
            last = (h, alpha[:, :1], probs.astype(BF16))
        add_product(*last)

    def place_of(r):
        return (zl + 3 - 2 * (r - 1) + 3 * ((r - 1) * (r - 2) // 2)) % 4

    send_group(0, zl)
    second_phase[0].wait()
    send_group(1, place_of(1))
    second_phase[1].wait()
    send_group(2, place_of(2))
    near_groups(0, zl)
    far_group(0, zl)
    attend(k, zl)
    second_phase[2].wait()
    second_phase[3].wait()
    send_group(3, place_of(3))

    def round_of(r, b_last):
        b = place_of(r)
        near_groups(r, b)
        shared(r - 1)
        attend(j, b_last)
        far_group(r, b)
        attend(k, b)
        return b

    b_last = lax.fori_loop(1, 4, round_of, zl)
    shared(3)
    attend(j, b_last)

    loads[5].wait()
    for h in range(HEADS):
        context = (acc[h] / l_ref[h][:, :1]).astype(BF16)
        hv[:, 128 * h : 128 * (h + 1)] = dot(context, wuv[h]).astype(BF16)
    hv_copy = remote(hv.at[pl.ds(pl.multiple_of(j * HALF, HALF), HALF)], hv_recv, hv_sem, sibling)
    hv_copy.start()

    number = lax.broadcasted_iota(jnp.int32, (1, 32), 1)
    sources = []
    for i in range(2):
        prompt = jnp.sum(jnp.where(slot_row[...] == 2 * c_idx + i, number, 0), axis=1, keepdims=True)
        held = jnp.sum(jnp.where(order_row[...] == prompt, number, 0), axis=1, keepdims=True)
        core, hx, hz = held & 1, held >> 3, (held >> 1) & 3
        row = row_id[:HALF]
        q, rest = row >> 5, row & 31
        zero = hz * 512 + q * 128 + hx * 32 + rest
        one = 2048 + hz * 512 + hx * 128 + q * 32 + rest
        sources.append(jnp.where(core == 0, zero, one))
    source = jnp.concatenate(sources, 0)
    key_lane = lax.broadcasted_iota(jnp.int32, (1, 1024), 1)
    picked_rows = jnp.zeros((ROWS, KVW), F32)
    for n in range(4):
        picked = jnp.where(key_lane + 1024 * n == source, 1.0, 0.0).astype(BF16)
        picked_rows = picked_rows + dot(picked, cache[1024 * n : 1024 * (n + 1), :])
    own_ref[...] = picked_rows.T.astype(BF16)

    loads[6].wait()
    wo_far.wait()
    hv_copy.wait()
    hv_own_rows = pl.ds(pl.multiple_of(k * HALF, HALF), HALF)

    up, down = device(dy=1), device(dy=-1)
    chunks = ((0, 0, 256), (0, 256, 256), (0, 512, 384), (1, 0, 512), (1, 512, 384))

    def partial(dy, n):
        s, first_column, width = chunks[n]
        zz = (1 - zh) * (1 - s) + zh * s
        start = (((y + dy + 4) % 4) * 2 + zz) * BLK + first_column
        columns = pl.ds(pl.multiple_of(start, 128), width)
        return dot(hv[hv_own_rows, :], wo[:, columns]) + dot(hv_recv[...], wo2[:, columns])

    def span(ref, n):
        s, first_column, width = chunks[n]
        return ref.at[s, :, pl.ds(first_column, width)]

    def far_out(n):
        p = partial(2, n).astype(BF16)
        for e, where in enumerate((up, down)):
            src = span(far_send.at[e], n)
            src[...] = p[64 * e : 64 * (e + 1)]
            remote(src, span(far_recv.at[e], n), far_sem.at[n, e], where).start()

    def near_copy(n, e, f, where):
        return remote(span(near_send.at[e, f], n), span(near_recv.at[e, f], n), near_sem.at[n, e, f], where)

    held = {}

    def near_out(n):
        for e, (dy, where) in enumerate(((1, up), (-1, down))):
            p = partial(dy, n)
            f = 1 - e
            span(near_send.at[e, f], n)[...] = p[64 * f : 64 * (f + 1)].astype(BF16)
            near_copy(n, e, f, where).start()
            held[n, e] = p[64 * e : 64 * (e + 1)]

    def near_added(n):
        for e, where in enumerate((up, down)):
            remote(span(far_send.at[e], n), span(far_recv.at[e], n), far_sem.at[n, e], where).wait()
            span(near_send.at[e, e], n)[...] = (
                held[n, e] + span(far_recv.at[e], n)[...].astype(F32)
            ).astype(BF16)
            near_copy(n, e, e, where).start()

    z_copies = []

    def finish(n):
        s, first_column, width = chunks[n]
        columns = pl.ds(first_column, width)
        p = partial(0, n)
        for e, where in enumerate((up, down)):
            for f in range(2):
                near_copy(n, e, f, where).wait()
        sums = [
            span(near_recv.at[0, f], n)[...].astype(F32) + span(near_recv.at[1, f], n)[...].astype(F32)
            for f in range(2)
        ]
        total = p + jnp.concatenate(sums, 0)
        if s == 0:
            zo_send[:, columns] = total.astype(BF16)
            cp = remote(zo_send.at[:, columns], zo_recv.at[:, columns], zo_sem.at[n], device(dz=4))
            cp.start()
            z_copies.append(cp)
            return
        for cp in z_copies[:2] if n == 3 else z_copies[2:]:
            cp.wait()
        fin[:, columns] = (total + zo_recv[:, columns].astype(F32)).astype(BF16)
        fin_copy(n).start()

    def fin_copy(n):
        columns = pl.ds(chunks[n][1], chunks[n][2])
        return remote(fin.at[:, columns], fin_recv.at[:, columns], fin_sem.at[n - 3], sibling)

    far_out(0)
    near_out(0)
    far_out(1)
    near_added(0)
    near_out(1)
    far_out(2)
    near_added(1)
    near_out(2)
    finish(0)
    far_out(3)
    near_added(2)
    near_out(3)
    finish(1)
    far_out(4)
    near_added(3)
    near_out(4)
    finish(2)
    near_added(4)
    finish(3)
    finish(4)
    mine_here = fin[...]
    mine_here = jnp.where(k == 0, mine_here[:, :448], mine_here[:, 448:])
    out_ref[:, hv_own_rows] = mine_here.T
    fin_copy(3).wait()
    fin_copy(4).wait()
    theirs = fin_recv[...]
    theirs = jnp.where(k == 0, theirs[:, :448], theirs[:, 448:])
    out_ref[:, pl.ds(pl.multiple_of(j * HALF, HALF), HALF)] = theirs.T
    for r in range(4):
        for i in range(2):
            remote(mine, mine, p3_sem.at[r, i], sibling).wait_send()
            remote(mine_half, mine_half, p4_sem.at[r, i], sibling).wait_send()
        for i in range(4):
            remote(mine, mine, sh_sem.at[r, i], sibling).wait_send()


def per_device(
    layer_input, q_latent, w_dkv, kv_gain, w_uq, w_uk, w_uv, w_o, block_order, owner_slot
):
    hbm = pl.BlockSpec(memory_space=pl.ANY)
    vmem = pl.BlockSpec(memory_space=pltpu.VMEM)
    smem = pl.BlockSpec(memory_space=pltpu.SMEM)
    V = pltpu.VMEM
    dma = pltpu.SemaphoreType.DMA
    out, own = pl.pallas_call(
        kernel,
        out_shape=(
            jax.ShapeDtypeStruct((448, ROWS), BF16),
            jax.ShapeDtypeStruct((KVW, ROWS), BF16),
        ),
        in_specs=[hbm, hbm, hbm, vmem, hbm, hbm, hbm, hbm, smem, vmem, vmem],
        out_specs=(vmem, vmem),
        scratch_shapes=[
            V((448, ROWS), BF16), V((ROWS, 1536), BF16), V((448, KVW), BF16), V((1536, 768), BF16),
            V((HEADS, LAT, NOPE), BF16), V((HEADS, LAT, NOPE), BF16), V((512, MODEL), BF16), V((512, MODEL), BF16),
            V((ROWS, KVW), F32), V((HALF, KVW), F32), V((HALF, KVW), F32), V((3, 32, KVW), F32),
            V((32, KVW), F32), V((32, KVW), F32),
            V((ROWS, 32), F32), V((ROWS, 32), F32), V((HEADS, ROWS, KVW), BF16), V((4096, KVW), BF16),
            V((HEADS, ROWS, 128), F32), V((HEADS, ROWS, 128), F32), V((HEADS, ROWS, LAT), F32),
            V((ROWS, 512), BF16), V((HALF, 512), BF16),
            V((2, 2, 64, BLK), BF16), V((2, 2, 64, BLK), BF16),
            V((2, 2, 2, 64, BLK), BF16), V((2, 2, 2, 64, BLK), BF16),
            V((HALF, BLK), BF16), V((HALF, BLK), BF16), V((HALF, BLK), BF16), V((HALF, BLK), BF16),
            dma((7,)), dma, dma, dma((2,)), dma((3, 2)), dma((2,)), dma((3, 2)), dma((4, 2)),
            dma((4, 2, 2)), dma((4, 2, 2)), dma((4, 4, 2)), dma((2,)), dma((5, 2, 2)), dma((5, 2, 2, 2)),
            dma((3, 2)), dma((2, 2)),
        ],
        compiler_params=pltpu.CompilerParams(
            collective_id=0, has_side_effects=True, vmem_limit_bytes=60 * 1024 * 1024
        ),
    )(
        layer_input.T, q_latent, w_dkv, kv_gain.reshape(1, LAT), w_uq, w_uk, w_uv, w_o,
        block_order, block_order.reshape(1, 32), owner_slot.reshape(1, 32),
    )
    return out.T, own.T


def solution(mesh):
    return jax.shard_map(
        per_device,
        mesh=mesh,
        in_specs=(
            P("ctx", "tp"),
            P("ctx", None),
            P("tp", None),
            P(),
            P(None, "tp"),
            P("tp", None, None),
            P("tp", None, None),
            P("tp", None),
            P(),
            P(),
        ),
        out_specs=(P("ctx", "tp"), P("ctx", None)),
        check_vma=False,
    )
```

```python
import functools
import math

import jax
import jax.numpy as jnp
from jax import lax
from jax.experimental import pallas as pl
from jax.experimental.pallas import tpu as pltpu
from jax.sharding import PartitionSpec as P

MESH = pl.DeviceIdType.MESH
F32 = jnp.float32
BF16 = jnp.bfloat16
ROWS = 256
HALF = 128
LAT = 512
ROPE = 64
KVW = 576
NOPE = 128
HEADS = 4
MODEL = 7168
BLK = 896
SCALE = 192.0 ** -0.5 * math.log2(math.e)


def dot(a, b):
    return jnp.dot(a, b, preferred_element_type=F32)


def dot_t(a, b):
    return lax.dot_general(a, b, (((1,), (1,)), ((), ())), preferred_element_type=F32)


def rope(v, cos, sin):
    a, b = v[:, :32], v[:, 32:64]
    return jnp.concatenate([a * cos - b * sin, a * sin + b * cos], 1)


def kernel(
    li_hbm, ql_hbm, wdkv_hbm, gain_ref, wuq_hbm, wuk_hbm, wuv_hbm, wo_hbm, order_ref, order_row, slot_row,
    out_ref, own_ref,
    li, ql, wdkv, wuq, wuk, wuv, wo, wo2,
    part, part_recv, ysum, yrecv, zsend, zrecv,
    cos_ref, sin_ref, queries, cache, m_ref, l_ref, acc,
    hv, hv_recv, far_send, far_recv, near_send, near_recv, zo_send, zo_recv, fin, fin_recv,
    ld_sem, wo_ssem, wo_rsem, p_sem, y_sem, z_sem, p1_sem, p2_sem, p3_sem, sh_sem,
    hv_sem, far_sem, near_sem, zo_sem, fin_sem,
):
    c_idx = lax.axis_index("ctx")
    t_idx = lax.axis_index("tp")
    x, zl = c_idx // 4, c_idx % 4
    y, zh, k = t_idx // 4, (t_idx // 2) % 2, t_idx % 2
    z = zh * 4 + zl
    j = 1 - k

    def device(dx=0, dy=0, dz=0, dk=0):
        nx, ny, nz, nk = (x + dx + 4) % 4, (y + dy + 4) % 4, (z + dz + 8) % 8, (k + dk) % 2
        return (nx * 4 + nz % 4, ny * 4 + (nz // 4) * 2 + nk)

    sibling = device(dk=1)

    def remote(src, dst, sem, where):
        copy = pltpu.make_async_remote_copy(
            src_ref=src, dst_ref=dst, send_sem=sem.at[0], recv_sem=sem.at[1],
            device_id=where, device_id_type=MESH,
        )
        return copy

    loads = []
    for i, (src, dst) in enumerate(
        ((li_hbm, li), (wdkv_hbm, wdkv), (ql_hbm, ql), (wuq_hbm, wuq), (wuk_hbm, wuk), (wuv_hbm, wuv), (wo_hbm, wo))
    ):
        loads.append(pltpu.make_async_copy(src, dst, ld_sem.at[i]))
    for copy in loads[:6]:
        copy.start()

    barrier = pltpu.get_barrier_semaphore()
    peers = [
        sibling, device(dy=1), device(dy=-1), device(dy=2), device(dz=4),
        device(dx=1), device(dx=-1), device(dx=2),
        device(dz=1), device(dz=-1), device(dz=2), device(dz=-2),
    ]
    for peer in peers:
        pl.semaphore_signal(barrier, inc=1, device_id=peer, device_id_type=MESH)

    row_id = lax.broadcasted_iota(jnp.int32, (ROWS, 1), 0)
    first, second = order_ref[2 * c_idx] * HALF, order_ref[2 * c_idx + 1] * HALF
    places = jnp.where(row_id < HALF, first + row_id, second + row_id - HALF)

    loads[0].wait()
    loads[1].wait()
    part[...] = lax.dot_general(li[...], wdkv[...], (((0,), (0,)), ((), ())), preferred_element_type=F32)
    pl.semaphore_wait(barrier, len(peers))
    cp = remote(part.at[pl.ds(pl.multiple_of(j * HALF, HALF), HALF)], part_recv, p_sem, sibling)
    cp.start()

    frequency = jnp.exp(
        lax.broadcasted_iota(jnp.int32, (1, 32), 1).astype(F32) * (-2.0 * math.log(10000.0) / ROPE)
    )
    angles = places.astype(F32) * frequency
    cos_ref[...] = jnp.cos(angles)
    sin_ref[...] = jnp.sin(angles)

    cp.wait()
    ysum[...] = part[pl.ds(pl.multiple_of(k * HALF, HALF), HALF), :] + part_recv[...]
    copies = []
    for i, d in enumerate((1, -1, 2)):
        ny = (y + d + 4) % 4
        cp = remote(
            ysum.at[pl.ds(pl.multiple_of(ny * 32, 32), 32)], yrecv.at[i], y_sem.at[i], device(dy=d)
        )
        cp.start()
        copies.append(cp)
    wo_far = pltpu.make_async_remote_copy(
        src_ref=wo_hbm, dst_ref=wo2, send_sem=wo_ssem, recv_sem=wo_rsem, device_id=sibling, device_id_type=MESH
    )
    wo_far.start()
    loads[6].start()

    loads[2].wait()
    loads[3].wait()
    q_proj = dot(ql[...], wuq[...])
    loads[4].wait()

    def absorb(h):
        q_nope = q_proj[:, 192 * h : 192 * h + NOPE].astype(BF16)
        queries[h, :, :LAT] = dot_t(q_nope, wuk[h]).astype(BF16)
        queries[h, :, LAT:] = rope(
            q_proj[:, 192 * h + NOPE : 192 * h + 192], cos_ref[...], sin_ref[...]
        ).astype(BF16)

    absorb(0)
    absorb(1)
    for cp in copies:
        cp.wait()
    zsend[...] = ((ysum[pl.ds(pl.multiple_of(y * 32, 32), 32), :] + yrecv[0]) + yrecv[1]) + yrecv[2]
    cp = remote(zsend, zrecv, z_sem, device(dz=4))
    cp.start()
    absorb(2)
    absorb(3)
    cp.wait()
    kv = zsend[...] + zrecv[...]
    latent = kv[:, :LAT]
    mean_square = jnp.mean(latent * latent, axis=1, keepdims=True)
    latent = latent * lax.rsqrt(mean_square + 1e-6) * gain_ref[...]
    own_row = pl.multiple_of(k * HALF + y * 32, 32)
    rotated = rope(kv[:, LAT:], cos_ref[pl.ds(own_row, 32), :], sin_ref[pl.ds(own_row, 32), :])

    a_own = x * j + y * k
    c_own = y * j + x * k

    def at(core, b, c, a=0, extra=0):
        return pl.multiple_of(core * 2048 + b * 512 + c * 128 + a * 32 + extra, 32)

    own_at = at(k, zl, c_own, a_own)
    cache[pl.ds(own_at, 32), :] = jnp.concatenate([latent, rotated], 1).astype(BF16)
    own_slab = cache.at[pl.ds(own_at, 32)]
    copies = []
    for i, d in enumerate((1, -1, 2)):
        cp = remote(own_slab, own_slab, p1_sem.at[i], device(dx=d * j, dy=d * k))
        cp.start()
        copies.append(cp)
    for cp in copies:
        cp.wait()

    def group(b, c):
        return cache.at[pl.ds(at(k, b, c), 128)]

    def half(b, c, e):
        return cache.at[pl.ds(at(k, b, c, 0, 64 * e), 64)]

    c_peers = (device(dy=j, dx=k), device(dy=-j, dx=-k), device(dy=2 * j, dx=2 * k))
    mine = group(zl, c_own)

    def share(r, i, src):
        remote(src, src, sh_sem.at[r, i], sibling).start()

    def send_group(r, b):
        src = group(b, c_own)
        for i, peer in enumerate(c_peers):
            remote(src, src, p3_sem.at[r, i], peer).start()
        share(r, 3, src)

    def receive(r, b):
        for i, d in enumerate((1, -1, 2)):
            remote(mine, mine, p3_sem.at[r, i], sibling).wait_recv()
            share(r, i, group(b, (c_own - d + 4) % 4))

    def shared(r):
        for i in range(4):
            remote(mine, mine, sh_sem.at[r, i], sibling).wait_recv()

    second_phase = []
    for i, (src, d) in enumerate(((mine, 1), (mine, -1), (half(zl, c_own, 0), 2), (half(zl, c_own, 1), -2))):
        cp = remote(src, src, p2_sem.at[i], device(dz=d))
        cp.start()
        second_phase.append(cp)

    lane = lax.broadcasted_iota(jnp.int32, (1, 128), 1)

    def bias_of(core, b):
        other = 1 - core
        pieces = []
        for c in range(4):
            held = []
            for a in range(4):
                ctx = 4 * (a * other + c * core) + b
                held.append(order_ref[2 * ctx + core] * HALF)
            base = jnp.where(
                lane < 64, jnp.where(lane < 32, held[0], held[1]), jnp.where(lane < 96, held[2], held[3])
            )
            pieces.append(base + lane % 32 + 32 * c * other + (lane // 32) * 32 * core)
        key_places = jnp.concatenate(pieces, 1)
        return jnp.where(key_places <= places, 0.0, -1e30)

    m_ref[...] = jnp.full(m_ref.shape, -1e29, F32)
    l_ref[...] = jnp.zeros(l_ref.shape, F32)
    acc[...] = jnp.zeros(acc.shape, F32)

    def attend(core, b):
        bias = bias_of(core, b)
        rows = pl.ds(at(core, b, 0), 512)

        def add_product(h, alpha, probs):
            acc[h] = acc[h] * alpha + dot(probs, cache[rows, :LAT])

        scores_next = dot_t(queries[0], cache[rows, :])
        last = None
        for h in range(HEADS):
            scores = scores_next
            if h + 1 < HEADS:
                scores_next = dot_t(queries[h + 1], cache[rows, :])
            if last is not None:
                add_product(*last)
            scores = scores * SCALE + bias
            m_old = m_ref[h]
            m_new = jnp.maximum(m_old, jnp.max(scores, axis=1, keepdims=True))
            alpha = jnp.exp2(m_old - m_new)
            probs = jnp.exp2(scores - m_new[:, :1])
            l_ref[h] = l_ref[h] * alpha + jnp.sum(probs, axis=1, keepdims=True)
            m_ref[h] = m_new
            last = (h, alpha[:, :1], probs.astype(BF16))
        add_product(*last)

    def place_of(r):
        return (zl + 3 - 2 * (r - 1) + 3 * ((r - 1) * (r - 2) // 2)) % 4

    send_group(0, zl)
    second_phase[0].wait()
    send_group(1, place_of(1))
    second_phase[1].wait()
    send_group(2, place_of(2))
    receive(0, zl)
    attend(k, zl)
    second_phase[2].wait()
    second_phase[3].wait()
    send_group(3, place_of(3))

    def round_of(r, b_last):
        b = place_of(r)
        shared(r - 1)
        attend(j, b_last)
        receive(r, b)
        attend(k, b)
        return b

    b_last = lax.fori_loop(1, 4, round_of, zl)
    shared(3)
    attend(j, b_last)

    loads[5].wait()
    for h in range(HEADS):
        context = (acc[h] / l_ref[h][:, :1]).astype(BF16)
        hv[:, 128 * h : 128 * (h + 1)] = dot(context, wuv[h]).astype(BF16)
    hv_copy = remote(hv.at[pl.ds(pl.multiple_of(j * HALF, HALF), HALF)], hv_recv, hv_sem, sibling)
    hv_copy.start()

    number = lax.broadcasted_iota(jnp.int32, (1, 32), 1)
    sources = []
    for i in range(2):
        prompt = jnp.sum(jnp.where(slot_row[...] == 2 * c_idx + i, number, 0), axis=1, keepdims=True)
        held = jnp.sum(jnp.where(order_row[...] == prompt, number, 0), axis=1, keepdims=True)
        core, hx, hz = held & 1, held >> 3, (held >> 1) & 3
        row = row_id[:HALF]
        q, rest = row >> 5, row & 31
        zero = hz * 512 + q * 128 + hx * 32 + rest
        one = 2048 + hz * 512 + hx * 128 + q * 32 + rest
        sources.append(jnp.where(core == 0, zero, one))
    source = jnp.concatenate(sources, 0)
    key_lane = lax.broadcasted_iota(jnp.int32, (1, 1024), 1)
    picked_rows = jnp.zeros((ROWS, KVW), F32)
    for n in range(4):
        picked = jnp.where(key_lane + 1024 * n == source, 1.0, 0.0).astype(BF16)
        picked_rows = picked_rows + dot(picked, cache[1024 * n : 1024 * (n + 1), :])
    own_ref[...] = picked_rows.T.astype(BF16)

    loads[6].wait()
    wo_far.wait()
    hv_copy.wait()
    hv_own_rows = pl.ds(pl.multiple_of(k * HALF, HALF), HALF)

    up, down = device(dy=1), device(dy=-1)
    chunks = ((0, 0, 256), (0, 256, 256), (0, 512, 384), (1, 0, 512), (1, 512, 384))

    def partial(dy, n):
        s, first_column, width = chunks[n]
        zz = (1 - zh) * (1 - s) + zh * s
        start = (((y + dy + 4) % 4) * 2 + zz) * BLK + first_column
        columns = pl.ds(pl.multiple_of(start, 128), width)
        return dot(hv[hv_own_rows, :], wo[:, columns]) + dot(hv_recv[...], wo2[:, columns])

    def span(ref, n):
        s, first_column, width = chunks[n]
        return ref.at[s, :, pl.ds(first_column, width)]

    def far_out(n):
        p = partial(2, n).astype(BF16)
        for e, where in enumerate((up, down)):
            src = span(far_send.at[e], n)
            src[...] = p[64 * e : 64 * (e + 1)]
            remote(src, span(far_recv.at[e], n), far_sem.at[n, e], where).start()

    def near_copy(n, e, f, where):
        return remote(span(near_send.at[e, f], n), span(near_recv.at[e, f], n), near_sem.at[n, e, f], where)

    held = {}

    def near_out(n):
        for e, (dy, where) in enumerate(((1, up), (-1, down))):
            p = partial(dy, n)
            f = 1 - e
            span(near_send.at[e, f], n)[...] = p[64 * f : 64 * (f + 1)].astype(BF16)
            near_copy(n, e, f, where).start()
            held[n, e] = p[64 * e : 64 * (e + 1)]

    def near_added(n):
        for e, where in enumerate((up, down)):
            remote(span(far_send.at[e], n), span(far_recv.at[e], n), far_sem.at[n, e], where).wait()
            span(near_send.at[e, e], n)[...] = (
                held[n, e] + span(far_recv.at[e], n)[...].astype(F32)
            ).astype(BF16)
            near_copy(n, e, e, where).start()

    z_copies = []

    def finish(n):
        s, first_column, width = chunks[n]
        columns = pl.ds(first_column, width)
        p = partial(0, n)
        for e, where in enumerate((up, down)):
            for f in range(2):
                near_copy(n, e, f, where).wait()
        sums = [
            span(near_recv.at[0, f], n)[...].astype(F32) + span(near_recv.at[1, f], n)[...].astype(F32)
            for f in range(2)
        ]
        total = p + jnp.concatenate(sums, 0)
        if s == 0:
            zo_send[:, columns] = total.astype(BF16)
            cp = remote(zo_send.at[:, columns], zo_recv.at[:, columns], zo_sem.at[n], device(dz=4))
            cp.start()
            z_copies.append(cp)
            return
        for cp in z_copies[:2] if n == 3 else z_copies[2:]:
            cp.wait()
        fin[:, columns] = (total + zo_recv[:, columns].astype(F32)).astype(BF16)
        fin_copy(n).start()

    def fin_copy(n):
        columns = pl.ds(chunks[n][1], chunks[n][2])
        return remote(fin.at[:, columns], fin_recv.at[:, columns], fin_sem.at[n - 3], sibling)

    far_out(0)
    near_out(0)
    far_out(1)
    near_added(0)
    near_out(1)
    far_out(2)
    near_added(1)
    near_out(2)
    finish(0)
    far_out(3)
    near_added(2)
    near_out(3)
    finish(1)
    far_out(4)
    near_added(3)
    near_out(4)
    finish(2)
    near_added(4)
    finish(3)
    finish(4)
    mine_here = fin[...]
    mine_here = jnp.where(k == 0, mine_here[:, :448], mine_here[:, 448:])
    out_ref[:, hv_own_rows] = mine_here.T
    fin_copy(3).wait()
    fin_copy(4).wait()
    theirs = fin_recv[...]
    theirs = jnp.where(k == 0, theirs[:, :448], theirs[:, 448:])
    out_ref[:, pl.ds(pl.multiple_of(j * HALF, HALF), HALF)] = theirs.T
    for r in range(4):
        for i in range(3):
            remote(mine, mine, p3_sem.at[r, i], sibling).wait_send()
        for i in range(4):
            remote(mine, mine, sh_sem.at[r, i], sibling).wait_send()


def per_device(
    layer_input, q_latent, w_dkv, kv_gain, w_uq, w_uk, w_uv, w_o, block_order, owner_slot
):
    hbm = pl.BlockSpec(memory_space=pl.ANY)
    vmem = pl.BlockSpec(memory_space=pltpu.VMEM)
    smem = pl.BlockSpec(memory_space=pltpu.SMEM)
    V = pltpu.VMEM
    dma = pltpu.SemaphoreType.DMA
    out, own = pl.pallas_call(
        kernel,
        out_shape=(
            jax.ShapeDtypeStruct((448, ROWS), BF16),
            jax.ShapeDtypeStruct((KVW, ROWS), BF16),
        ),
        in_specs=[hbm, hbm, hbm, vmem, hbm, hbm, hbm, hbm, smem, vmem, vmem],
        out_specs=(vmem, vmem),
        scratch_shapes=[
            V((448, ROWS), BF16), V((ROWS, 1536), BF16), V((448, KVW), BF16), V((1536, 768), BF16),
            V((HEADS, LAT, NOPE), BF16), V((HEADS, LAT, NOPE), BF16), V((512, MODEL), BF16), V((512, MODEL), BF16),
            V((ROWS, KVW), F32), V((HALF, KVW), F32), V((HALF, KVW), F32), V((3, 32, KVW), F32),
            V((32, KVW), F32), V((32, KVW), F32),
            V((ROWS, 32), F32), V((ROWS, 32), F32), V((HEADS, ROWS, KVW), BF16), V((4096, KVW), BF16),
            V((HEADS, ROWS, 128), F32), V((HEADS, ROWS, 128), F32), V((HEADS, ROWS, LAT), F32),
            V((ROWS, 512), BF16), V((HALF, 512), BF16),
            V((2, 2, 64, BLK), BF16), V((2, 2, 64, BLK), BF16),
            V((2, 2, 2, 64, BLK), BF16), V((2, 2, 2, 64, BLK), BF16),
            V((HALF, BLK), BF16), V((HALF, BLK), BF16), V((HALF, BLK), BF16), V((HALF, BLK), BF16),
            dma((7,)), dma, dma, dma((2,)), dma((3, 2)), dma((2,)), dma((3, 2)), dma((4, 2)),
            dma((4, 3, 2)), dma((4, 4, 2)), dma((2,)), dma((5, 2, 2)), dma((5, 2, 2, 2)),
            dma((3, 2)), dma((2, 2)),
        ],
        compiler_params=pltpu.CompilerParams(
            collective_id=0, has_side_effects=True, vmem_limit_bytes=60 * 1024 * 1024
        ),
    )(
        layer_input.T, q_latent, w_dkv, kv_gain.reshape(1, LAT), w_uq, w_uk, w_uv, w_o,
        block_order, block_order.reshape(1, 32), owner_slot.reshape(1, 32),
    )
    return out.T, own.T


def solution(mesh):
    return jax.shard_map(
        per_device,
        mesh=mesh,
        in_specs=(
            P("ctx", "tp"),
            P("ctx", None),
            P("tp", None),
            P(),
            P(None, "tp"),
            P("tp", None, None),
            P("tp", None, None),
            P("tp", None),
            P(),
            P(),
        ),
        out_specs=(P("ctx", "tp"), P("ctx", None)),
        check_vma=False,
    )
```

```python
import functools
import math

import jax
import jax.numpy as jnp
from jax import lax
from jax.experimental import pallas as pl
from jax.experimental.pallas import tpu as pltpu
from jax.sharding import PartitionSpec as P

MESH = pl.DeviceIdType.MESH
F32 = jnp.float32
BF16 = jnp.bfloat16
ROWS = 256
HALF = 128
LAT = 512
ROPE = 64
KVW = 576
NOPE = 128
HEADS = 4
MODEL = 7168
BLK = 896
SCALE = 192.0 ** -0.5 * math.log2(math.e)


def dot(a, b):
    return jnp.dot(a, b, preferred_element_type=F32)


def dot_t(a, b):
    return lax.dot_general(a, b, (((1,), (1,)), ((), ())), preferred_element_type=F32)


def rope(v, cos, sin):
    a, b = v[:, :32], v[:, 32:64]
    return jnp.concatenate([a * cos - b * sin, a * sin + b * cos], 1)


def kernel(
    li_hbm, ql_hbm, wdkv_hbm, gain_ref, wuq_hbm, wuk_hbm, wuv_hbm, wo_hbm, order_ref, order_row, slot_row,
    out_ref, own_ref,
    li, ql, wdkv, wuq, wuk, wuv, wo, wo2,
    part, part_recv, ysum, yrecv, zsend, zrecv,
    cos_ref, sin_ref, queries, cache, m_ref, l_ref, acc,
    hv, hv_recv, far_send, far_recv, near_send, near_recv, direct_send, direct_recv, zo_send, zo_recv, fin, fin_recv,
    ld_sem, wo_ssem, wo_rsem, p_sem, y_sem, z_sem, p1_sem, p2_sem, p3_sem, sh_sem,
    hv_sem, far_sem, near_sem, direct_sem, zo_sem, fin_sem,
):
    c_idx = lax.axis_index("ctx")
    t_idx = lax.axis_index("tp")
    x, zl = c_idx // 4, c_idx % 4
    y, zh, k = t_idx // 4, (t_idx // 2) % 2, t_idx % 2
    z = zh * 4 + zl
    j = 1 - k

    def device(dx=0, dy=0, dz=0, dk=0):
        nx, ny, nz, nk = (x + dx + 4) % 4, (y + dy + 4) % 4, (z + dz + 8) % 8, (k + dk) % 2
        return (nx * 4 + nz % 4, ny * 4 + (nz // 4) * 2 + nk)

    sibling = device(dk=1)

    def remote(src, dst, sem, where):
        copy = pltpu.make_async_remote_copy(
            src_ref=src, dst_ref=dst, send_sem=sem.at[0], recv_sem=sem.at[1],
            device_id=where, device_id_type=MESH,
        )
        return copy

    loads = []
    for i, (src, dst) in enumerate(
        ((li_hbm, li), (wdkv_hbm, wdkv), (ql_hbm, ql), (wuq_hbm, wuq), (wuk_hbm, wuk), (wuv_hbm, wuv), (wo_hbm, wo))
    ):
        loads.append(pltpu.make_async_copy(src, dst, ld_sem.at[i]))
    for copy in loads[:6]:
        copy.start()

    barrier = pltpu.get_barrier_semaphore()
    peers = [
        sibling, device(dy=1), device(dy=-1), device(dy=2), device(dz=4),
        device(dx=1), device(dx=-1), device(dx=2),
        device(dz=1), device(dz=-1), device(dz=2), device(dz=-2),
    ]
    for peer in peers:
        pl.semaphore_signal(barrier, inc=1, device_id=peer, device_id_type=MESH)

    row_id = lax.broadcasted_iota(jnp.int32, (ROWS, 1), 0)
    first, second = order_ref[2 * c_idx] * HALF, order_ref[2 * c_idx + 1] * HALF
    places = jnp.where(row_id < HALF, first + row_id, second + row_id - HALF)

    loads[0].wait()
    loads[1].wait()
    part[...] = lax.dot_general(li[...], wdkv[...], (((0,), (0,)), ((), ())), preferred_element_type=F32)
    pl.semaphore_wait(barrier, len(peers))
    cp = remote(part.at[pl.ds(pl.multiple_of(j * HALF, HALF), HALF)], part_recv, p_sem, sibling)
    cp.start()

    frequency = jnp.exp(
        lax.broadcasted_iota(jnp.int32, (1, 32), 1).astype(F32) * (-2.0 * math.log(10000.0) / ROPE)
    )
    angles = places.astype(F32) * frequency
    cos_ref[...] = jnp.cos(angles)
    sin_ref[...] = jnp.sin(angles)

    cp.wait()
    ysum[...] = part[pl.ds(pl.multiple_of(k * HALF, HALF), HALF), :] + part_recv[...]
    copies = []
    for i, d in enumerate((1, -1, 2)):
        ny = (y + d + 4) % 4
        cp = remote(
            ysum.at[pl.ds(pl.multiple_of(ny * 32, 32), 32)], yrecv.at[i], y_sem.at[i], device(dy=d)
        )
        cp.start()
        copies.append(cp)
    wo_far = pltpu.make_async_remote_copy(
        src_ref=wo_hbm, dst_ref=wo2, send_sem=wo_ssem, recv_sem=wo_rsem, device_id=sibling, device_id_type=MESH
    )
    wo_far.start()
    loads[6].start()

    loads[2].wait()
    loads[3].wait()
    q_proj = dot(ql[...], wuq[...])
    loads[4].wait()

    def absorb(h):
        q_nope = q_proj[:, 192 * h : 192 * h + NOPE].astype(BF16)
        queries[h, :, :LAT] = dot_t(q_nope, wuk[h]).astype(BF16)
        queries[h, :, LAT:] = rope(
            q_proj[:, 192 * h + NOPE : 192 * h + 192], cos_ref[...], sin_ref[...]
        ).astype(BF16)

    absorb(0)
    absorb(1)
    for cp in copies:
        cp.wait()
    zsend[...] = ((ysum[pl.ds(pl.multiple_of(y * 32, 32), 32), :] + yrecv[0]) + yrecv[1]) + yrecv[2]
    cp = remote(zsend, zrecv, z_sem, device(dz=4))
    cp.start()
    absorb(2)
    absorb(3)
    cp.wait()
    kv = zsend[...] + zrecv[...]
    latent = kv[:, :LAT]
    mean_square = jnp.mean(latent * latent, axis=1, keepdims=True)
    latent = latent * lax.rsqrt(mean_square + 1e-6) * gain_ref[...]
    own_row = pl.multiple_of(k * HALF + y * 32, 32)
    rotated = rope(kv[:, LAT:], cos_ref[pl.ds(own_row, 32), :], sin_ref[pl.ds(own_row, 32), :])

    a_own = x * j + y * k
    c_own = y * j + x * k

    def at(core, b, c, a=0, extra=0):
        return pl.multiple_of(core * 2048 + b * 512 + c * 128 + a * 32 + extra, 32)

    own_at = at(k, zl, c_own, a_own)
    cache[pl.ds(own_at, 32), :] = jnp.concatenate([latent, rotated], 1).astype(BF16)
    own_slab = cache.at[pl.ds(own_at, 32)]
    copies = []
    for i, d in enumerate((1, -1, 2)):
        cp = remote(own_slab, own_slab, p1_sem.at[i], device(dx=d * j, dy=d * k))
        cp.start()
        copies.append(cp)
    for cp in copies:
        cp.wait()

    def group(b, c):
        return cache.at[pl.ds(at(k, b, c), 128)]

    def half(b, c, e):
        return cache.at[pl.ds(at(k, b, c, 0, 64 * e), 64)]

    c_peers = (device(dy=j, dx=k), device(dy=-j, dx=-k), device(dy=2 * j, dx=2 * k))
    mine = group(zl, c_own)

    def share(r, i, src):
        remote(src, src, sh_sem.at[r, i], sibling).start()

    def send_group(r, b):
        src = group(b, c_own)
        for i, peer in enumerate(c_peers):
            remote(src, src, p3_sem.at[r, i], peer).start()
        share(r, 3, src)

    def receive(r, b):
        for i, d in enumerate((1, -1, 2)):
            remote(mine, mine, p3_sem.at[r, i], sibling).wait_recv()
            share(r, i, group(b, (c_own - d + 4) % 4))

    def shared(r):
        for i in range(4):
            remote(mine, mine, sh_sem.at[r, i], sibling).wait_recv()

    second_phase = []
    for i, (src, d) in enumerate(((mine, 1), (mine, -1), (half(zl, c_own, 0), 2), (half(zl, c_own, 1), -2))):
        cp = remote(src, src, p2_sem.at[i], device(dz=d))
        cp.start()
        second_phase.append(cp)

    lane = lax.broadcasted_iota(jnp.int32, (1, 128), 1)

    def bias_of(core, b):
        other = 1 - core
        pieces = []
        for c in range(4):
            held = []
            for a in range(4):
                ctx = 4 * (a * other + c * core) + b
                held.append(order_ref[2 * ctx + core] * HALF)
            base = jnp.where(
                lane < 64, jnp.where(lane < 32, held[0], held[1]), jnp.where(lane < 96, held[2], held[3])
            )
            pieces.append(base + lane % 32 + 32 * c * other + (lane // 32) * 32 * core)
        key_places = jnp.concatenate(pieces, 1)
        return jnp.where(key_places <= places, 0.0, -1e30)

    m_ref[...] = jnp.full(m_ref.shape, -1e29, F32)
    l_ref[...] = jnp.zeros(l_ref.shape, F32)
    acc[...] = jnp.zeros(acc.shape, F32)

    def attend(core, b):
        bias = bias_of(core, b)
        rows = pl.ds(at(core, b, 0), 512)

        def add_product(h, alpha, probs):
            acc[h] = acc[h] * alpha + dot(probs, cache[rows, :LAT])

        scores_next = dot_t(queries[0], cache[rows, :])
        last = None
        for h in range(HEADS):
            scores = scores_next
            if h + 1 < HEADS:
                scores_next = dot_t(queries[h + 1], cache[rows, :])
            if last is not None:
                add_product(*last)
            scores = scores * SCALE + bias
            m_old = m_ref[h]
            m_new = jnp.maximum(m_old, jnp.max(scores, axis=1, keepdims=True))
            alpha = jnp.exp2(m_old - m_new)
            probs = jnp.exp2(scores - m_new[:, :1])
            l_ref[h] = l_ref[h] * alpha + jnp.sum(probs, axis=1, keepdims=True)
            m_ref[h] = m_new
            last = (h, alpha[:, :1], probs.astype(BF16))
        add_product(*last)

    def place_of(r):
        return (zl + 3 - 2 * (r - 1) + 3 * ((r - 1) * (r - 2) // 2)) % 4

    send_group(0, zl)
    second_phase[0].wait()
    send_group(1, place_of(1))
    second_phase[1].wait()
    send_group(2, place_of(2))
    receive(0, zl)
    attend(k, zl)
    second_phase[2].wait()
    second_phase[3].wait()
    send_group(3, place_of(3))

    def round_of(r, b_last):
        b = place_of(r)
        shared(r - 1)
        attend(j, b_last)
        receive(r, b)
        attend(k, b)
        return b

    b_last = lax.fori_loop(1, 4, round_of, zl)
    shared(3)
    attend(j, b_last)

    loads[5].wait()

    def head_values(rows):
        for h in range(HEADS):
            context = (acc[h, rows, :] / l_ref[h, rows, :1]).astype(BF16)
            hv[rows, 128 * h : 128 * (h + 1)] = dot(context, wuv[h]).astype(BF16)

    hv_own_rows = pl.ds(pl.multiple_of(k * HALF, HALF), HALF)
    hv_sibling_rows = pl.ds(pl.multiple_of(j * HALF, HALF), HALF)
    head_values(hv_sibling_rows)
    hv_copy = remote(hv.at[hv_sibling_rows], hv_recv, hv_sem, sibling)
    hv_copy.start()
    head_values(hv_own_rows)
    loads[6].wait()
    wo_far.wait()
    hv_copy.wait()

    up, down = device(dy=1), device(dy=-1)
    chunks = ((0, 0, 256), (0, 256, 256), (0, 512, 384), (1, 0, 512), (1, 512, 384))

    def partial(dy, n):
        s, first_column, width = chunks[n]
        zz = (1 - zh) * (1 - s) + zh * s
        start = (((y + dy + 4) % 4) * 2 + zz) * BLK + first_column
        columns = pl.ds(pl.multiple_of(start, 128), width)
        return dot(hv[hv_own_rows, :], wo[:, columns]) + dot(hv_recv[...], wo2[:, columns])

    def span(ref, n):
        s, first_column, width = chunks[n]
        return ref.at[s, :, pl.ds(first_column, width)]

    def far_out(n):
        p = partial(2, n).astype(BF16)
        for e, where in enumerate((up, down)):
            src = span(far_send.at[e], n)
            src[...] = p[64 * e : 64 * (e + 1)]
            remote(src, span(far_recv.at[e], n), far_sem.at[n, e], where).start()

    def near_copy(n, e, f, where):
        return remote(span(near_send.at[e, f], n), span(near_recv.at[e, f], n), near_sem.at[n, e, f], where)

    direct_peers = ((1, up), (-1, down), (2, device(dy=2)))

    def direct_copy(i, where):
        return remote(direct_send.at[i], direct_recv.at[i], direct_sem.at[i], where)

    def direct_out():
        for i, (dy, where) in enumerate(direct_peers):
            direct_send[i] = partial(dy, 0).astype(BF16)
            direct_copy(i, where).start()

    held = {}

    def near_out(n):
        for e, (dy, where) in enumerate(((1, up), (-1, down))):
            p = partial(dy, n)
            f = 1 - e
            span(near_send.at[e, f], n)[...] = p[64 * f : 64 * (f + 1)].astype(BF16)
            near_copy(n, e, f, where).start()
            held[n, e] = p[64 * e : 64 * (e + 1)]

    def near_added(n):
        for e, where in enumerate((up, down)):
            remote(span(far_send.at[e], n), span(far_recv.at[e], n), far_sem.at[n, e], where).wait()
            span(near_send.at[e, e], n)[...] = (
                held[n, e] + span(far_recv.at[e], n)[...].astype(F32)
            ).astype(BF16)
            near_copy(n, e, e, where).start()

    z_copies = []

    def finish(n):
        s, first_column, width = chunks[n]
        columns = pl.ds(first_column, width)
        total = partial(0, n)
        if n == 0:
            for i, (_, where) in enumerate(direct_peers):
                direct_copy(i, where).wait()
                total = total + direct_recv[i].astype(F32)
        else:
            for e, where in enumerate((up, down)):
                for f in range(2):
                    near_copy(n, e, f, where).wait()
            sums = [
                span(near_recv.at[0, f], n)[...].astype(F32) + span(near_recv.at[1, f], n)[...].astype(F32)
                for f in range(2)
            ]
            total = total + jnp.concatenate(sums, 0)
        if s == 0:
            zo_send[:, columns] = total.astype(BF16)
            cp = remote(zo_send.at[:, columns], zo_recv.at[:, columns], zo_sem.at[n], device(dz=4))
            cp.start()
            z_copies.append(cp)
            return
        for cp in z_copies[:2] if n == 3 else z_copies[2:]:
            cp.wait()
        fin[:, columns] = (total + zo_recv[:, columns].astype(F32)).astype(BF16)
        fin_copy(n).start()

    def fin_copy(n):
        columns = pl.ds(chunks[n][1], chunks[n][2])
        return remote(fin.at[:, columns], fin_recv.at[:, columns], fin_sem.at[n - 3], sibling)

    def pick_owned():
        number = lax.broadcasted_iota(jnp.int32, (1, 32), 1)
        sources = []
        for i in range(2):
            prompt = jnp.sum(jnp.where(slot_row[...] == 2 * c_idx + i, number, 0), axis=1, keepdims=True)
            held = jnp.sum(jnp.where(order_row[...] == prompt, number, 0), axis=1, keepdims=True)
            core, hx, hz = held & 1, held >> 3, (held >> 1) & 3
            row = row_id[:HALF]
            q, rest = row >> 5, row & 31
            zero = hz * 512 + q * 128 + hx * 32 + rest
            one = 2048 + hz * 512 + hx * 128 + q * 32 + rest
            sources.append(jnp.where(core == 0, zero, one))
        source = jnp.concatenate(sources, 0)
        key_lane = lax.broadcasted_iota(jnp.int32, (1, 1024), 1)
        picked_rows = jnp.zeros((ROWS, KVW), F32)
        for n in range(4):
            picked = jnp.where(key_lane + 1024 * n == source, 1.0, 0.0).astype(BF16)
            picked_rows = picked_rows + dot(picked, cache[1024 * n : 1024 * (n + 1), :])
        own_ref[...] = picked_rows.T.astype(BF16)

    far_out(1)
    direct_out()
    near_out(1)
    far_out(2)
    near_out(2)
    near_added(1)
    finish(0)
    near_added(2)
    far_out(3)
    near_out(3)
    finish(1)
    far_out(4)
    near_out(4)
    near_added(3)
    pick_owned()
    finish(2)
    near_added(4)
    finish(3)
    finish(4)
    out_ref[hv_own_rows, :] = fin[...]
    fin_copy(3).wait()
    fin_copy(4).wait()
    out_ref[hv_sibling_rows, :] = fin_recv[...]
    for r in range(4):
        for i in range(3):
            remote(mine, mine, p3_sem.at[r, i], sibling).wait_send()
        for i in range(4):
            remote(mine, mine, sh_sem.at[r, i], sibling).wait_send()


def per_device(
    layer_input, q_latent, w_dkv, kv_gain, w_uq, w_uk, w_uv, w_o, block_order, owner_slot
):
    hbm = pl.BlockSpec(memory_space=pl.ANY)
    vmem = pl.BlockSpec(memory_space=pltpu.VMEM)
    smem = pl.BlockSpec(memory_space=pltpu.SMEM)
    V = pltpu.VMEM
    dma = pltpu.SemaphoreType.DMA
    out, own = pl.pallas_call(
        kernel,
        out_shape=(
            jax.ShapeDtypeStruct((ROWS, BLK), BF16),
            jax.ShapeDtypeStruct((KVW, ROWS), BF16),
        ),
        in_specs=[hbm, hbm, hbm, vmem, hbm, hbm, hbm, hbm, smem, vmem, vmem],
        out_specs=(vmem, vmem),
        scratch_shapes=[
            V((448, ROWS), BF16), V((ROWS, 1536), BF16), V((448, KVW), BF16), V((1536, 768), BF16),
            V((HEADS, LAT, NOPE), BF16), V((HEADS, LAT, NOPE), BF16), V((512, MODEL), BF16), V((512, MODEL), BF16),
            V((ROWS, KVW), F32), V((HALF, KVW), F32), V((HALF, KVW), F32), V((3, 32, KVW), F32),
            V((32, KVW), F32), V((32, KVW), F32),
            V((ROWS, 32), F32), V((ROWS, 32), F32), V((HEADS, ROWS, KVW), BF16), V((4096, KVW), BF16),
            V((HEADS, ROWS, 128), F32), V((HEADS, ROWS, 128), F32), V((HEADS, ROWS, LAT), F32),
            V((ROWS, 512), BF16), V((HALF, 512), BF16),
            V((2, 2, 64, BLK), BF16), V((2, 2, 64, BLK), BF16),
            V((2, 2, 2, 64, BLK), BF16), V((2, 2, 2, 64, BLK), BF16),
            V((3, HALF, 256), BF16), V((3, HALF, 256), BF16),
            V((HALF, BLK), BF16), V((HALF, BLK), BF16), V((HALF, BLK), BF16), V((HALF, BLK), BF16),
            dma((7,)), dma, dma, dma((2,)), dma((3, 2)), dma((2,)), dma((3, 2)), dma((4, 2)),
            dma((4, 3, 2)), dma((4, 4, 2)), dma((2,)), dma((5, 2, 2)), dma((5, 2, 2, 2)),
            dma((3, 2)),
            dma((3, 2)), dma((2, 2)),
        ],
        compiler_params=pltpu.CompilerParams(
            collective_id=0, has_side_effects=True, vmem_limit_bytes=60 * 1024 * 1024
        ),
    )(
        layer_input.T, q_latent, w_dkv, kv_gain.reshape(1, LAT), w_uq, w_uk, w_uv, w_o,
        block_order, block_order.reshape(1, 32), owner_slot.reshape(1, 32),
    )

    def hand_over(block, owned, out_ref, own_ref):
        core = lax.axis_index("tp") % 2
        block = block[...]
        out_ref[...] = jnp.where(core == 0, block[:, :448], block[:, 448:]).T
        own_ref[...] = owned[...]

    out, own = pl.pallas_call(
        hand_over,
        out_shape=(
            jax.ShapeDtypeStruct((448, ROWS), BF16),
            jax.ShapeDtypeStruct((KVW, ROWS), BF16),
        ),
        in_specs=[vmem, vmem],
        out_specs=(vmem, vmem),
    )(out, own)
    return out.T, own.T


def solution(mesh):
    return jax.shard_map(
        per_device,
        mesh=mesh,
        in_specs=(
            P("ctx", "tp"),
            P("ctx", None),
            P("tp", None),
            P(),
            P(None, "tp"),
            P("tp", None, None),
            P("tp", None, None),
            P("tp", None),
            P(),
            P(),
        ),
        out_specs=(P("ctx", "tp"), P("ctx", None)),
        check_vma=False,
    )
```

```python
import functools
import math

import jax
import jax.numpy as jnp
from jax import lax
from jax.experimental import pallas as pl
from jax.experimental.pallas import tpu as pltpu
from jax.sharding import PartitionSpec as P

MESH = pl.DeviceIdType.MESH
F32 = jnp.float32
BF16 = jnp.bfloat16
ROWS = 256
HALF = 128
LAT = 512
ROPE = 64
KVW = 576
NOPE = 128
HEADS = 4
MODEL = 7168
BLK = 896
SCALE = 192.0 ** -0.5 * math.log2(math.e)


def dot(a, b):
    return jnp.dot(a, b, preferred_element_type=F32)


def dot_t(a, b):
    return lax.dot_general(a, b, (((1,), (1,)), ((), ())), preferred_element_type=F32)


def rope(v, cos, sin):
    a, b = v[:, :32], v[:, 32:64]
    return jnp.concatenate([a * cos - b * sin, a * sin + b * cos], 1)


def kernel(
    li_hbm, ql_hbm, wdkv_hbm, gain_ref, wuq_hbm, wuk_hbm, wuv_hbm, wo_hbm, order_ref, order_row, slot_row,
    out_ref, own_ref,
    li, ql, wdkv, wuq, wuk, wuv, wo, wo2,
    part, part_recv, ysum, yrecv, zsend, zrecv,
    cos_ref, sin_ref, queries, cache, m_ref, l_ref, acc,
    hv, hv_recv, far_send, far_recv, near_send, near_recv, direct_send, direct_recv, zo_send, zo_recv, fin, fin_recv,
    ld_sem, wo_ssem, wo_rsem, p_sem, y_sem, z_sem, p1_sem, p2_sem, p3_sem, sh_sem,
    hv_sem, far_sem, near_sem, direct_sem, zo_sem, fin_sem,
):
    c_idx = lax.axis_index("ctx")
    t_idx = lax.axis_index("tp")
    x, zl = c_idx // 4, c_idx % 4
    y, zh, k = t_idx // 4, (t_idx // 2) % 2, t_idx % 2
    z = zh * 4 + zl
    j = 1 - k

    def device(dx=0, dy=0, dz=0, dk=0):
        nx, ny, nz, nk = (x + dx + 4) % 4, (y + dy + 4) % 4, (z + dz + 8) % 8, (k + dk) % 2
        return (nx * 4 + nz % 4, ny * 4 + (nz // 4) * 2 + nk)

    sibling = device(dk=1)

    def remote(src, dst, sem, where):
        copy = pltpu.make_async_remote_copy(
            src_ref=src, dst_ref=dst, send_sem=sem.at[0], recv_sem=sem.at[1],
            device_id=where, device_id_type=MESH,
        )
        return copy

    loads = []
    for i, (src, dst) in enumerate(
        ((li_hbm, li), (wdkv_hbm, wdkv), (ql_hbm, ql), (wuq_hbm, wuq), (wuk_hbm, wuk), (wuv_hbm, wuv), (wo_hbm, wo))
    ):
        loads.append(pltpu.make_async_copy(src, dst, ld_sem.at[i]))
    for copy in loads[:6]:
        copy.start()

    barrier = pltpu.get_barrier_semaphore()
    peers = [
        sibling, device(dy=1), device(dy=-1), device(dy=2), device(dz=4),
        device(dx=1), device(dx=-1), device(dx=2),
        device(dz=1), device(dz=-1),
    ]
    for peer in peers:
        pl.semaphore_signal(barrier, inc=1, device_id=peer, device_id_type=MESH)

    row_id = lax.broadcasted_iota(jnp.int32, (ROWS, 1), 0)
    first, second = order_ref[2 * c_idx] * HALF, order_ref[2 * c_idx + 1] * HALF
    places = jnp.where(row_id < HALF, first + row_id, second + row_id - HALF)

    loads[0].wait()
    loads[1].wait()
    part[...] = lax.dot_general(li[...], wdkv[...], (((0,), (0,)), ((), ())), preferred_element_type=F32)
    pl.semaphore_wait(barrier, len(peers))
    cp = remote(part.at[pl.ds(pl.multiple_of(j * HALF, HALF), HALF)], part_recv, p_sem, sibling)
    cp.start()

    frequency = jnp.exp(
        lax.broadcasted_iota(jnp.int32, (1, 32), 1).astype(F32) * (-2.0 * math.log(10000.0) / ROPE)
    )
    angles = places.astype(F32) * frequency
    cos_ref[...] = jnp.cos(angles)
    sin_ref[...] = jnp.sin(angles)

    cp.wait()
    ysum[...] = part[pl.ds(pl.multiple_of(k * HALF, HALF), HALF), :] + part_recv[...]
    copies = []
    for i, d in enumerate((1, -1, 2)):
        ny = (y + d + 4) % 4
        cp = remote(
            ysum.at[pl.ds(pl.multiple_of(ny * 32, 32), 32)], yrecv.at[i], y_sem.at[i], device(dy=d)
        )
        cp.start()
        copies.append(cp)
    wo_far = pltpu.make_async_remote_copy(
        src_ref=wo_hbm, dst_ref=wo2, send_sem=wo_ssem, recv_sem=wo_rsem, device_id=sibling, device_id_type=MESH
    )
    wo_far.start()
    loads[6].start()

    loads[2].wait()
    loads[3].wait()
    q_proj = dot(ql[...], wuq[...])
    loads[4].wait()

    def absorb(h):
        q_nope = q_proj[:, 192 * h : 192 * h + NOPE].astype(BF16)
        queries[h, :, :LAT] = dot_t(q_nope, wuk[h]).astype(BF16)
        queries[h, :, LAT:] = rope(
            q_proj[:, 192 * h + NOPE : 192 * h + 192], cos_ref[...], sin_ref[...]
        ).astype(BF16)

    absorb(0)
    absorb(1)
    for cp in copies:
        cp.wait()
    zsend[...] = ((ysum[pl.ds(pl.multiple_of(y * 32, 32), 32), :] + yrecv[0]) + yrecv[1]) + yrecv[2]
    cp = remote(zsend, zrecv, z_sem, device(dz=4))
    cp.start()
    absorb(2)
    absorb(3)
    cp.wait()
    kv = zsend[...] + zrecv[...]
    latent = kv[:, :LAT]
    mean_square = jnp.mean(latent * latent, axis=1, keepdims=True)
    latent = latent * lax.rsqrt(mean_square + 1e-6) * gain_ref[...]
    own_row = pl.multiple_of(k * HALF + y * 32, 32)
    rotated = rope(kv[:, LAT:], cos_ref[pl.ds(own_row, 32), :], sin_ref[pl.ds(own_row, 32), :])

    a_own = x * j + y * k
    c_own = y * j + x * k

    def at(core, b, c, a=0, extra=0):
        return pl.multiple_of(core * 2048 + b * 512 + c * 128 + a * 32 + extra, 32)

    own_at = at(k, zl, c_own, a_own)
    cache[pl.ds(own_at, 32), :] = jnp.concatenate([latent, rotated], 1).astype(BF16)
    own_slab = cache.at[pl.ds(own_at, 32)]
    copies = []
    for i, d in enumerate((1, -1, 2)):
        cp = remote(own_slab, own_slab, p1_sem.at[i], device(dx=d * j, dy=d * k))
        cp.start()
        copies.append(cp)
    for cp in copies:
        cp.wait()

    def group(b, c):
        return cache.at[pl.ds(at(k, b, c), 128)]

    def half(b, c, e):
        return cache.at[pl.ds(at(k, b, c, 0, 64 * e), 64)]

    c_peers = (device(dy=j, dx=k), device(dy=-j, dx=-k), device(dy=2 * j, dx=2 * k))
    mine = group(zl, c_own)

    def share(r, i, src):
        remote(src, src, sh_sem.at[r, i], sibling).start()

    def send_group(r, b):
        src = group(b, c_own)
        for i, peer in enumerate(c_peers):
            remote(src, src, p3_sem.at[r, i], peer).start()
        share(r, 3, src)

    def receive(r, b):
        for i, d in enumerate((1, -1, 2)):
            remote(mine, mine, p3_sem.at[r, i], sibling).wait_recv()
            share(r, i, group(b, (c_own - d + 4) % 4))

    def shared(r):
        for i in range(4):
            remote(mine, mine, sh_sem.at[r, i], sibling).wait_recv()

    second_phase = []
    for i, d in enumerate((1, -1)):
        cp = remote(mine, mine, p2_sem.at[i], device(dz=d))
        cp.start()
        second_phase.append(cp)

    lane = lax.broadcasted_iota(jnp.int32, (1, 128), 1)

    def bias_of(core, b):
        other = 1 - core
        pieces = []
        for c in range(4):
            held = []
            for a in range(4):
                ctx = 4 * (a * other + c * core) + b
                held.append(order_ref[2 * ctx + core] * HALF)
            base = jnp.where(
                lane < 64, jnp.where(lane < 32, held[0], held[1]), jnp.where(lane < 96, held[2], held[3])
            )
            pieces.append(base + lane % 32 + 32 * c * other + (lane // 32) * 32 * core)
        key_places = jnp.concatenate(pieces, 1)
        return jnp.where(key_places <= places, 0.0, -1e30)

    m_ref[...] = jnp.full(m_ref.shape, -1e29, F32)
    l_ref[...] = jnp.zeros(l_ref.shape, F32)
    acc[...] = jnp.zeros(acc.shape, F32)

    def attend(core, b):
        bias = bias_of(core, b)
        rows = pl.ds(at(core, b, 0), 512)

        def add_product(h, alpha, probs):
            acc[h] = acc[h] * alpha + dot(probs, cache[rows, :LAT])

        scores_next = dot_t(queries[0], cache[rows, :])
        last = None
        for h in range(HEADS):
            scores = scores_next
            if h + 1 < HEADS:
                scores_next = dot_t(queries[h + 1], cache[rows, :])
            if last is not None:
                add_product(*last)
            scores = scores * SCALE + bias
            m_old = m_ref[h]
            m_new = jnp.maximum(m_old, jnp.max(scores, axis=1, keepdims=True))
            alpha = jnp.exp2(m_old - m_new)
            probs = jnp.exp2(scores - m_new[:, :1])
            l_ref[h] = l_ref[h] * alpha + jnp.sum(probs, axis=1, keepdims=True)
            m_ref[h] = m_new
            last = (h, alpha[:, :1], probs.astype(BF16))
        add_product(*last)

    def place_of(r):
        return (zl + 3 - 2 * (r - 1) + 3 * ((r - 1) * (r - 2) // 2)) % 4

    send_group(0, zl)
    for i, d in enumerate((1, -1)):
        b = place_of(i + 1)
        second_phase[i].wait()
        forwarded = half(b, c_own, i)
        cp = remote(forwarded, forwarded, p2_sem.at[i + 2], device(dz=d))
        cp.start()
        second_phase.append(cp)
        send_group(i + 1, b)
    receive(0, zl)
    attend(k, zl)
    second_phase[2].wait()
    second_phase[3].wait()
    send_group(3, place_of(3))

    def round_of(r, b_last):
        b = place_of(r)
        shared(r - 1)
        attend(j, b_last)
        receive(r, b)
        attend(k, b)
        return b

    b_last = lax.fori_loop(1, 4, round_of, zl)
    shared(3)
    attend(j, b_last)

    loads[5].wait()

    def head_values(rows):
        for h in range(HEADS):
            context = (acc[h, rows, :] / l_ref[h, rows, :1]).astype(BF16)
            hv[rows, 128 * h : 128 * (h + 1)] = dot(context, wuv[h]).astype(BF16)

    hv_own_rows = pl.ds(pl.multiple_of(k * HALF, HALF), HALF)
    hv_sibling_rows = pl.ds(pl.multiple_of(j * HALF, HALF), HALF)
    head_values(hv_sibling_rows)
    hv_copy = remote(hv.at[hv_sibling_rows], hv_recv, hv_sem, sibling)
    hv_copy.start()
    head_values(hv_own_rows)
    loads[6].wait()
    wo_far.wait()
    hv_copy.wait()

    up, down = device(dy=1), device(dy=-1)
    chunks = ((0, 0, 256), (0, 256, 256), (0, 512, 384), (1, 0, 512), (1, 512, 384))

    def partial(dy, n):
        s, first_column, width = chunks[n]
        zz = (1 - zh) * (1 - s) + zh * s
        start = (((y + dy + 4) % 4) * 2 + zz) * BLK + first_column
        columns = pl.ds(pl.multiple_of(start, 128), width)
        return dot(hv[hv_own_rows, :], wo[:, columns]) + dot(hv_recv[...], wo2[:, columns])

    def span(ref, n):
        s, first_column, width = chunks[n]
        return ref.at[s, :, pl.ds(first_column, width)]

    def far_out(n):
        p = partial(2, n).astype(BF16)
        for e, where in enumerate((up, down)):
            src = span(far_send.at[e], n)
            src[...] = p[64 * e : 64 * (e + 1)]
            remote(src, span(far_recv.at[e], n), far_sem.at[n, e], where).start()

    def near_copy(n, e, f, where):
        return remote(span(near_send.at[e, f], n), span(near_recv.at[e, f], n), near_sem.at[n, e, f], where)

    direct_peers = ((1, up), (-1, down), (2, device(dy=2)))

    def direct_copy(i, where):
        return remote(direct_send.at[i], direct_recv.at[i], direct_sem.at[i], where)

    def direct_out():
        for i, (dy, where) in enumerate(direct_peers):
            direct_send[i] = partial(dy, 0).astype(BF16)
            direct_copy(i, where).start()

    held = {}

    def near_out(n):
        for e, (dy, where) in enumerate(((1, up), (-1, down))):
            p = partial(dy, n)
            f = 1 - e
            span(near_send.at[e, f], n)[...] = p[64 * f : 64 * (f + 1)].astype(BF16)
            near_copy(n, e, f, where).start()
            held[n, e] = p[64 * e : 64 * (e + 1)]

    def near_added(n):
        for e, where in enumerate((up, down)):
            remote(span(far_send.at[e], n), span(far_recv.at[e], n), far_sem.at[n, e], where).wait()
            span(near_send.at[e, e], n)[...] = (
                held[n, e] + span(far_recv.at[e], n)[...].astype(F32)
            ).astype(BF16)
            near_copy(n, e, e, where).start()

    z_copies = []

    def finish(n):
        s, first_column, width = chunks[n]
        columns = pl.ds(first_column, width)
        total = partial(0, n)
        if n == 0:
            for i, (_, where) in enumerate(direct_peers):
                direct_copy(i, where).wait()
                total = total + direct_recv[i].astype(F32)
        else:
            for e, where in enumerate((up, down)):
                for f in range(2):
                    near_copy(n, e, f, where).wait()
            sums = [
                span(near_recv.at[0, f], n)[...].astype(F32) + span(near_recv.at[1, f], n)[...].astype(F32)
                for f in range(2)
            ]
            total = total + jnp.concatenate(sums, 0)
        if s == 0:
            zo_send[:, columns] = total.astype(BF16)
            cp = remote(zo_send.at[:, columns], zo_recv.at[:, columns], zo_sem.at[n], device(dz=4))
            cp.start()
            z_copies.append(cp)
            return
        for cp in z_copies[:2] if n == 3 else z_copies[2:]:
            cp.wait()
        fin[:, columns] = (total + zo_recv[:, columns].astype(F32)).astype(BF16)
        fin_copy(n).start()

    def fin_copy(n):
        columns = pl.ds(chunks[n][1], chunks[n][2])
        return remote(fin.at[:, columns], fin_recv.at[:, columns], fin_sem.at[n - 3], sibling)

    def pick_owned():
        number = lax.broadcasted_iota(jnp.int32, (1, 32), 1)
        sources = []
        for i in range(2):
            prompt = jnp.sum(jnp.where(slot_row[...] == 2 * c_idx + i, number, 0), axis=1, keepdims=True)
            held = jnp.sum(jnp.where(order_row[...] == prompt, number, 0), axis=1, keepdims=True)
            core, hx, hz = held & 1, held >> 3, (held >> 1) & 3
            row = row_id[:HALF]
            q, rest = row >> 5, row & 31
            zero = hz * 512 + q * 128 + hx * 32 + rest
            one = 2048 + hz * 512 + hx * 128 + q * 32 + rest
            sources.append(jnp.where(core == 0, zero, one))
        source = jnp.concatenate(sources, 0)
        key_lane = lax.broadcasted_iota(jnp.int32, (1, 1024), 1)
        picked_rows = jnp.zeros((ROWS, KVW), F32)
        for n in range(4):
            picked = jnp.where(key_lane + 1024 * n == source, 1.0, 0.0).astype(BF16)
            picked_rows = picked_rows + dot(picked, cache[1024 * n : 1024 * (n + 1), :])
        own_ref[...] = picked_rows.T.astype(BF16)

    far_out(1)
    direct_out()
    near_out(1)
    far_out(2)
    near_out(2)
    near_added(1)
    finish(0)
    near_added(2)
    far_out(3)
    far_out(4)
    near_out(3)
    finish(1)
    near_out(4)
    near_added(3)
    finish(2)
    near_added(4)
    pick_owned()
    finish(3)
    finish(4)
    out_ref[hv_own_rows, :] = fin[...]
    fin_copy(3).wait()
    fin_copy(4).wait()
    out_ref[hv_sibling_rows, :] = fin_recv[...]
    for r in range(4):
        for i in range(3):
            remote(mine, mine, p3_sem.at[r, i], sibling).wait_send()
        for i in range(4):
            remote(mine, mine, sh_sem.at[r, i], sibling).wait_send()


def per_device(
    layer_input, q_latent, w_dkv, kv_gain, w_uq, w_uk, w_uv, w_o, block_order, owner_slot
):
    hbm = pl.BlockSpec(memory_space=pl.ANY)
    vmem = pl.BlockSpec(memory_space=pltpu.VMEM)
    smem = pl.BlockSpec(memory_space=pltpu.SMEM)
    V = pltpu.VMEM
    dma = pltpu.SemaphoreType.DMA
    out, own = pl.pallas_call(
        kernel,
        out_shape=(
            jax.ShapeDtypeStruct((ROWS, BLK), BF16),
            jax.ShapeDtypeStruct((KVW, ROWS), BF16),
        ),
        in_specs=[hbm, hbm, hbm, vmem, hbm, hbm, hbm, hbm, smem, vmem, vmem],
        out_specs=(vmem, vmem),
        scratch_shapes=[
            V((448, ROWS), BF16), V((ROWS, 1536), BF16), V((448, KVW), BF16), V((1536, 768), BF16),
            V((HEADS, LAT, NOPE), BF16), V((HEADS, LAT, NOPE), BF16), V((512, MODEL), BF16), V((512, MODEL), BF16),
            V((ROWS, KVW), F32), V((HALF, KVW), F32), V((HALF, KVW), F32), V((3, 32, KVW), F32),
            V((32, KVW), F32), V((32, KVW), F32),
            V((ROWS, 32), F32), V((ROWS, 32), F32), V((HEADS, ROWS, KVW), BF16), V((4096, KVW), BF16),
            V((HEADS, ROWS, 128), F32), V((HEADS, ROWS, 128), F32), V((HEADS, ROWS, LAT), F32),
            V((ROWS, 512), BF16), V((HALF, 512), BF16),
            V((2, 2, 64, BLK), BF16), V((2, 2, 64, BLK), BF16),
            V((2, 2, 2, 64, BLK), BF16), V((2, 2, 2, 64, BLK), BF16),
            V((3, HALF, 256), BF16), V((3, HALF, 256), BF16),
            V((HALF, BLK), BF16), V((HALF, BLK), BF16), V((HALF, BLK), BF16), V((HALF, BLK), BF16),
            dma((7,)), dma, dma, dma((2,)), dma((3, 2)), dma((2,)), dma((3, 2)), dma((4, 2)),
            dma((4, 3, 2)), dma((4, 4, 2)), dma((2,)), dma((5, 2, 2)), dma((5, 2, 2, 2)),
            dma((3, 2)),
            dma((3, 2)), dma((2, 2)),
        ],
        compiler_params=pltpu.CompilerParams(
            collective_id=0, has_side_effects=True, vmem_limit_bytes=60 * 1024 * 1024
        ),
    )(
        layer_input.T, q_latent, w_dkv, kv_gain.reshape(1, LAT), w_uq, w_uk, w_uv, w_o,
        block_order, block_order.reshape(1, 32), owner_slot.reshape(1, 32),
    )

    def hand_over(block, owned, out_ref, own_ref):
        core = lax.axis_index("tp") % 2
        block = block[...]
        out_ref[...] = jnp.where(core == 0, block[:, :448], block[:, 448:]).T
        own_ref[...] = owned[...]

    out, own = pl.pallas_call(
        hand_over,
        out_shape=(
            jax.ShapeDtypeStruct((448, ROWS), BF16),
            jax.ShapeDtypeStruct((KVW, ROWS), BF16),
        ),
        in_specs=[vmem, vmem],
        out_specs=(vmem, vmem),
    )(out, own)
    return out.T, own.T


def solution(mesh):
    return jax.shard_map(
        per_device,
        mesh=mesh,
        in_specs=(
            P("ctx", "tp"),
            P("ctx", None),
            P("tp", None),
            P(),
            P(None, "tp"),
            P("tp", None, None),
            P("tp", None, None),
            P("tp", None),
            P(),
            P(),
        ),
        out_specs=(P("ctx", "tp"), P("ctx", None)),
        check_vma=False,
    )
```

```python
import functools
import math

import jax
import jax.numpy as jnp
from jax import lax
from jax.experimental import pallas as pl
from jax.experimental.pallas import tpu as pltpu
from jax.sharding import PartitionSpec as P

MESH = pl.DeviceIdType.MESH
F32 = jnp.float32
BF16 = jnp.bfloat16
ROWS = 256
HALF = 128
LAT = 512
ROPE = 64
KVW = 576
NOPE = 128
HEADS = 4
MODEL = 7168
BLK = 896
SCALE = 192.0 ** -0.5 * math.log2(math.e)


def dot(a, b):
    return jnp.dot(a, b, preferred_element_type=F32)


def dot_t(a, b):
    return lax.dot_general(a, b, (((1,), (1,)), ((), ())), preferred_element_type=F32)


def rope(v, cos, sin):
    a, b = v[:, :32], v[:, 32:64]
    return jnp.concatenate([a * cos - b * sin, a * sin + b * cos], 1)


def kernel(
    li_hbm, ql_hbm, wdkv_hbm, gain_ref, wuq_hbm, wuk_hbm, wuv_hbm, wo_hbm, order_ref, order_row, slot_row,
    out_hbm, own_hbm,
    li, ql, wdkv, wuq, wuk, wuv, wo, wo2,
    part, part_recv, ysum, yrecv, zsend, zrecv,
    cos_ref, sin_ref, queries, cache, m_ref, l_ref, acc,
    hv, hv_recv, far_send, far_recv, near_send, near_recv, direct_send, direct_recv, zo_send, zo_recv, fin, fin_recv,
    out_ref, own_ref, out_sem, ld_sem, wo_ssem, wo_rsem, p_sem, y_sem, z_sem, p1_sem, p2_sem, p3_sem, sh_sem,
    hv_sem, far_sem, near_sem, direct_sem, zo_sem, fin_sem,
):
    c_idx = lax.axis_index("ctx")
    t_idx = lax.axis_index("tp")
    x, zl = c_idx // 4, c_idx % 4
    y, zh, k = t_idx // 4, (t_idx // 2) % 2, t_idx % 2
    z = zh * 4 + zl
    j = 1 - k

    def device(dx=0, dy=0, dz=0, dk=0):
        nx, ny, nz, nk = (x + dx + 4) % 4, (y + dy + 4) % 4, (z + dz + 8) % 8, (k + dk) % 2
        return (nx * 4 + nz % 4, ny * 4 + (nz // 4) * 2 + nk)

    sibling = device(dk=1)

    def remote(src, dst, sem, where):
        copy = pltpu.make_async_remote_copy(
            src_ref=src, dst_ref=dst, send_sem=sem.at[0], recv_sem=sem.at[1],
            device_id=where, device_id_type=MESH,
        )
        return copy

    loads = []
    for i, (src, dst) in enumerate(
        ((li_hbm, li), (wdkv_hbm, wdkv), (ql_hbm, ql), (wuq_hbm, wuq), (wuk_hbm, wuk), (wuv_hbm, wuv), (wo_hbm, wo))
    ):
        loads.append(pltpu.make_async_copy(src, dst, ld_sem.at[i]))
    for copy in loads[:6]:
        copy.start()

    barrier = pltpu.get_barrier_semaphore()
    peers = [
        sibling, device(dy=1), device(dy=-1), device(dy=2), device(dz=4),
        device(dx=1), device(dx=-1), device(dx=2),
        device(dz=1), device(dz=-1),
    ]
    for peer in peers:
        pl.semaphore_signal(barrier, inc=1, device_id=peer, device_id_type=MESH)

    row_id = lax.broadcasted_iota(jnp.int32, (ROWS, 1), 0)
    first, second = order_ref[2 * c_idx] * HALF, order_ref[2 * c_idx + 1] * HALF
    places = jnp.where(row_id < HALF, first + row_id, second + row_id - HALF)

    loads[0].wait()
    loads[1].wait()
    part[...] = lax.dot_general(li[...], wdkv[...], (((0,), (0,)), ((), ())), preferred_element_type=F32)
    pl.semaphore_wait(barrier, len(peers))
    cp = remote(part.at[pl.ds(pl.multiple_of(j * HALF, HALF), HALF)], part_recv, p_sem, sibling)
    cp.start()

    frequency = jnp.exp(
        lax.broadcasted_iota(jnp.int32, (1, 32), 1).astype(F32) * (-2.0 * math.log(10000.0) / ROPE)
    )
    angles = places.astype(F32) * frequency
    cos_ref[...] = jnp.cos(angles)
    sin_ref[...] = jnp.sin(angles)

    cp.wait()
    ysum[...] = part[pl.ds(pl.multiple_of(k * HALF, HALF), HALF), :] + part_recv[...]
    copies = []
    for i, d in enumerate((1, -1, 2)):
        ny = (y + d + 4) % 4
        cp = remote(
            ysum.at[pl.ds(pl.multiple_of(ny * 32, 32), 32)], yrecv.at[i], y_sem.at[i], device(dy=d)
        )
        cp.start()
        copies.append(cp)
    wo_far = pltpu.make_async_remote_copy(
        src_ref=wo_hbm, dst_ref=wo2, send_sem=wo_ssem, recv_sem=wo_rsem, device_id=sibling, device_id_type=MESH
    )
    wo_far.start()
    loads[6].start()

    loads[2].wait()
    loads[3].wait()
    q_proj = dot(ql[...], wuq[...])
    loads[4].wait()

    def absorb(h):
        q_nope = q_proj[:, 192 * h : 192 * h + NOPE].astype(BF16)
        queries[h, :, :LAT] = dot_t(q_nope, wuk[h]).astype(BF16)
        queries[h, :, LAT:] = rope(
            q_proj[:, 192 * h + NOPE : 192 * h + 192], cos_ref[...], sin_ref[...]
        ).astype(BF16)

    absorb(0)
    absorb(1)
    for cp in copies:
        cp.wait()
    zsend[...] = ((ysum[pl.ds(pl.multiple_of(y * 32, 32), 32), :] + yrecv[0]) + yrecv[1]) + yrecv[2]
    cp = remote(zsend, zrecv, z_sem, device(dz=4))
    cp.start()
    absorb(2)
    absorb(3)
    cp.wait()
    kv = zsend[...] + zrecv[...]
    latent = kv[:, :LAT]
    mean_square = jnp.mean(latent * latent, axis=1, keepdims=True)
    latent = latent * lax.rsqrt(mean_square + 1e-6) * gain_ref[...]
    own_row = pl.multiple_of(k * HALF + y * 32, 32)
    rotated = rope(kv[:, LAT:], cos_ref[pl.ds(own_row, 32), :], sin_ref[pl.ds(own_row, 32), :])

    a_own = x * j + y * k
    c_own = y * j + x * k

    def at(core, b, c, a=0, extra=0):
        return pl.multiple_of(core * 2048 + b * 512 + c * 128 + a * 32 + extra, 32)

    own_at = at(k, zl, c_own, a_own)
    cache[pl.ds(own_at, 32), :] = jnp.concatenate([latent, rotated], 1).astype(BF16)
    own_slab = cache.at[pl.ds(own_at, 32)]
    copies = []
    for i, d in enumerate((1, -1, 2)):
        cp = remote(own_slab, own_slab, p1_sem.at[i], device(dx=d * j, dy=d * k))
        cp.start()
        copies.append(cp)
    for cp in copies:
        cp.wait()

    def group(b, c):
        return cache.at[pl.ds(at(k, b, c), 128)]

    def half(b, c, e):
        return cache.at[pl.ds(at(k, b, c, 0, 64 * e), 64)]

    c_peers = (device(dy=j, dx=k), device(dy=-j, dx=-k), device(dy=2 * j, dx=2 * k))
    mine = group(zl, c_own)

    def share(r, i, src):
        remote(src, src, sh_sem.at[r, i], sibling).start()

    def send_group(r, b):
        src = group(b, c_own)
        for i, peer in enumerate(c_peers):
            remote(src, src, p3_sem.at[r, i], peer).start()
        share(r, 3, src)

    def receive(r, b):
        for i, d in enumerate((1, -1, 2)):
            remote(mine, mine, p3_sem.at[r, i], sibling).wait_recv()
            share(r, i, group(b, (c_own - d + 4) % 4))

    def shared(r):
        for i in range(4):
            remote(mine, mine, sh_sem.at[r, i], sibling).wait_recv()

    second_phase = []
    for i, d in enumerate((1, -1)):
        cp = remote(mine, mine, p2_sem.at[i], device(dz=d))
        cp.start()
        second_phase.append(cp)

    lane = lax.broadcasted_iota(jnp.int32, (1, 128), 1)

    def bias_of(core, b):
        other = 1 - core
        pieces = []
        for c in range(4):
            held = []
            for a in range(4):
                ctx = 4 * (a * other + c * core) + b
                held.append(order_ref[2 * ctx + core] * HALF)
            base = jnp.where(
                lane < 64, jnp.where(lane < 32, held[0], held[1]), jnp.where(lane < 96, held[2], held[3])
            )
            pieces.append(base + lane % 32 + 32 * c * other + (lane // 32) * 32 * core)
        key_places = jnp.concatenate(pieces, 1)
        return jnp.where(key_places <= places, 0.0, -1e30)

    m_ref[...] = jnp.full(m_ref.shape, -1e29, F32)
    l_ref[...] = jnp.zeros(l_ref.shape, F32)
    acc[...] = jnp.zeros(acc.shape, F32)

    def attend(core, b):
        bias = bias_of(core, b)
        rows = pl.ds(at(core, b, 0), 512)

        def add_product(h, alpha, probs):
            acc[h] = acc[h] * alpha + dot(probs, cache[rows, :LAT])

        scores_next = dot_t(queries[0], cache[rows, :])
        last = None
        for h in range(HEADS):
            scores = scores_next
            if h + 1 < HEADS:
                scores_next = dot_t(queries[h + 1], cache[rows, :])
            if last is not None:
                add_product(*last)
            scores = scores * SCALE + bias
            m_old = m_ref[h]
            m_new = jnp.maximum(m_old, jnp.max(scores, axis=1, keepdims=True))
            alpha = jnp.exp2(m_old - m_new)
            probs = jnp.exp2(scores - m_new[:, :1])
            l_ref[h] = l_ref[h] * alpha + jnp.sum(probs, axis=1, keepdims=True)
            m_ref[h] = m_new
            last = (h, alpha[:, :1], probs.astype(BF16))
        add_product(*last)

    def place_of(r):
        return (zl + 3 - 2 * (r - 1) + 3 * ((r - 1) * (r - 2) // 2)) % 4

    send_group(0, zl)
    for i, d in enumerate((1, -1)):
        b = place_of(i + 1)
        second_phase[i].wait()
        forwarded = half(b, c_own, i)
        cp = remote(forwarded, forwarded, p2_sem.at[i + 2], device(dz=d))
        cp.start()
        second_phase.append(cp)
        send_group(i + 1, b)
    receive(0, zl)
    attend(k, zl)
    second_phase[2].wait()
    second_phase[3].wait()
    send_group(3, place_of(3))

    def round_of(r, b_last):
        b = place_of(r)
        shared(r - 1)
        attend(j, b_last)
        receive(r, b)
        attend(k, b)
        return b

    b_last = lax.fori_loop(1, 4, round_of, zl)
    shared(3)
    attend(j, b_last)

    loads[5].wait()

    def head_values(rows):
        for h in range(HEADS):
            context = (acc[h, rows, :] / l_ref[h, rows, :1]).astype(BF16)
            hv[rows, 128 * h : 128 * (h + 1)] = dot(context, wuv[h]).astype(BF16)

    hv_own_rows = pl.ds(pl.multiple_of(k * HALF, HALF), HALF)
    hv_sibling_rows = pl.ds(pl.multiple_of(j * HALF, HALF), HALF)
    head_values(hv_sibling_rows)
    hv_copy = remote(hv.at[hv_sibling_rows], hv_recv, hv_sem, sibling)
    hv_copy.start()
    head_values(hv_own_rows)
    loads[6].wait()
    wo_far.wait()
    hv_copy.wait()

    up, down = device(dy=1), device(dy=-1)
    chunks = ((0, 0, 256), (0, 256, 256), (0, 512, 384), (1, 0, 512), (1, 512, 384))

    def partial(dy, n):
        s, first_column, width = chunks[n]
        zz = (1 - zh) * (1 - s) + zh * s
        start = (((y + dy + 4) % 4) * 2 + zz) * BLK + first_column
        columns = pl.ds(pl.multiple_of(start, 128), width)
        return dot(hv[hv_own_rows, :], wo[:, columns]) + dot(hv_recv[...], wo2[:, columns])

    def span(ref, n):
        s, first_column, width = chunks[n]
        return ref.at[s, :, pl.ds(first_column, width)]

    def far_out(n):
        p = partial(2, n).astype(BF16)
        for e, where in enumerate((up, down)):
            src = span(far_send.at[e], n)
            src[...] = p[64 * e : 64 * (e + 1)]
            remote(src, span(far_recv.at[e], n), far_sem.at[n, e], where).start()

    def near_copy(n, e, f, where):
        return remote(span(near_send.at[e, f], n), span(near_recv.at[e, f], n), near_sem.at[n, e, f], where)

    direct_peers = ((1, up), (-1, down), (2, device(dy=2)))

    def direct_copy(i, where):
        return remote(direct_send.at[i], direct_recv.at[i], direct_sem.at[i], where)

    def direct_out():
        for i, (dy, where) in enumerate(direct_peers):
            direct_send[i] = partial(dy, 0).astype(BF16)
            direct_copy(i, where).start()

    held = {}

    def near_out(n):
        for e, (dy, where) in enumerate(((1, up), (-1, down))):
            p = partial(dy, n)
            f = 1 - e
            span(near_send.at[e, f], n)[...] = p[64 * f : 64 * (f + 1)].astype(BF16)
            near_copy(n, e, f, where).start()
            held[n, e] = p[64 * e : 64 * (e + 1)]

    def near_added(n):
        for e, where in enumerate((up, down)):
            remote(span(far_send.at[e], n), span(far_recv.at[e], n), far_sem.at[n, e], where).wait()
            span(near_send.at[e, e], n)[...] = (
                held[n, e] + span(far_recv.at[e], n)[...].astype(F32)
            ).astype(BF16)
            near_copy(n, e, e, where).start()

    z_copies = []

    def finish(n):
        s, first_column, width = chunks[n]
        columns = pl.ds(first_column, width)
        total = partial(0, n)
        if n == 0:
            for i, (_, where) in enumerate(direct_peers):
                direct_copy(i, where).wait()
                total = total + direct_recv[i].astype(F32)
        else:
            for e, where in enumerate((up, down)):
                for f in range(2):
                    near_copy(n, e, f, where).wait()
            sums = [
                span(near_recv.at[0, f], n)[...].astype(F32) + span(near_recv.at[1, f], n)[...].astype(F32)
                for f in range(2)
            ]
            total = total + jnp.concatenate(sums, 0)
        if s == 0:
            zo_send[:, columns] = total.astype(BF16)
            cp = remote(zo_send.at[:, columns], zo_recv.at[:, columns], zo_sem.at[n], device(dz=4))
            cp.start()
            z_copies.append(cp)
            return
        for cp in z_copies[:2] if n == 3 else z_copies[2:]:
            cp.wait()
        fin[:, columns] = (total + zo_recv[:, columns].astype(F32)).astype(BF16)
        fin_copy(n).start()

    def fin_copy(n):
        columns = pl.ds(chunks[n][1], chunks[n][2])
        return remote(fin.at[:, columns], fin_recv.at[:, columns], fin_sem.at[n - 3], sibling)

    def pick_owned():
        number = lax.broadcasted_iota(jnp.int32, (1, 32), 1)
        sources = []
        for i in range(2):
            prompt = jnp.sum(jnp.where(slot_row[...] == 2 * c_idx + i, number, 0), axis=1, keepdims=True)
            held = jnp.sum(jnp.where(order_row[...] == prompt, number, 0), axis=1, keepdims=True)
            core, hx, hz = held & 1, held >> 3, (held >> 1) & 3
            row = row_id[:HALF]
            q, rest = row >> 5, row & 31
            zero = hz * 512 + q * 128 + hx * 32 + rest
            one = 2048 + hz * 512 + hx * 128 + q * 32 + rest
            sources.append(jnp.where(core == 0, zero, one))
        source = jnp.concatenate(sources, 0)
        key_lane = lax.broadcasted_iota(jnp.int32, (1, 1024), 1)
        picked_rows = jnp.zeros((ROWS, KVW), F32)
        for n in range(4):
            picked = jnp.where(key_lane + 1024 * n == source, 1.0, 0.0).astype(BF16)
            picked_rows = picked_rows + dot(picked, cache[1024 * n : 1024 * (n + 1), :])
        own_ref[...] = picked_rows.T.astype(BF16)
        pltpu.make_async_copy(own_ref, own_hbm, out_sem.at[0]).start()

    far_out(1)
    direct_out()
    near_out(1)
    far_out(2)
    near_out(2)
    near_added(1)
    finish(0)
    near_added(2)
    far_out(3)
    far_out(4)
    near_out(3)
    finish(1)
    near_out(4)
    near_added(3)
    finish(2)
    near_added(4)
    pick_owned()
    finish(3)
    finish(4)
    pltpu.make_async_copy(fin, out_hbm.at[hv_own_rows], out_sem.at[1]).start()
    fin_copy(3).wait()
    fin_copy(4).wait()
    pltpu.make_async_copy(fin_recv, out_hbm.at[hv_sibling_rows], out_sem.at[2]).start()
    for r in range(4):
        for i in range(3):
            remote(mine, mine, p3_sem.at[r, i], sibling).wait_send()
        for i in range(4):
            remote(mine, mine, sh_sem.at[r, i], sibling).wait_send()
    pltpu.make_async_copy(own_ref, own_hbm, out_sem.at[0]).wait()
    pltpu.make_async_copy(fin, out_hbm.at[hv_own_rows], out_sem.at[1]).wait()
    pltpu.make_async_copy(fin_recv, out_hbm.at[hv_sibling_rows], out_sem.at[2]).wait()


def per_device(
    layer_input, q_latent, w_dkv, kv_gain, w_uq, w_uk, w_uv, w_o, block_order, owner_slot
):
    hbm = pl.BlockSpec(memory_space=pl.ANY)
    vmem = pl.BlockSpec(memory_space=pltpu.VMEM)
    smem = pl.BlockSpec(memory_space=pltpu.SMEM)
    V = pltpu.VMEM
    dma = pltpu.SemaphoreType.DMA
    out, own = pl.pallas_call(
        kernel,
        out_shape=(
            jax.ShapeDtypeStruct((ROWS, BLK), BF16),
            jax.ShapeDtypeStruct((KVW, ROWS), BF16),
        ),
        in_specs=[hbm, hbm, hbm, vmem, hbm, hbm, hbm, hbm, smem, vmem, vmem],
        out_specs=(hbm, hbm),
        scratch_shapes=[
            V((448, ROWS), BF16), V((ROWS, 1536), BF16), V((448, KVW), BF16), V((1536, 768), BF16),
            V((HEADS, LAT, NOPE), BF16), V((HEADS, LAT, NOPE), BF16), V((512, MODEL), BF16), V((512, MODEL), BF16),
            V((ROWS, KVW), F32), V((HALF, KVW), F32), V((HALF, KVW), F32), V((3, 32, KVW), F32),
            V((32, KVW), F32), V((32, KVW), F32),
            V((ROWS, 32), F32), V((ROWS, 32), F32), V((HEADS, ROWS, KVW), BF16), V((4096, KVW), BF16),
            V((HEADS, ROWS, 128), F32), V((HEADS, ROWS, 128), F32), V((HEADS, ROWS, LAT), F32),
            V((ROWS, 512), BF16), V((HALF, 512), BF16),
            V((2, 2, 64, BLK), BF16), V((2, 2, 64, BLK), BF16),
            V((2, 2, 2, 64, BLK), BF16), V((2, 2, 2, 64, BLK), BF16),
            V((3, HALF, 256), BF16), V((3, HALF, 256), BF16),
            V((HALF, BLK), BF16), V((HALF, BLK), BF16), V((HALF, BLK), BF16), V((HALF, BLK), BF16),
            V((ROWS, BLK), BF16), V((KVW, ROWS), BF16), dma((3,)), dma((7,)), dma, dma, dma((2,)), dma((3, 2)), dma((2,)), dma((3, 2)), dma((4, 2)),
            dma((4, 3, 2)), dma((4, 4, 2)), dma((2,)), dma((5, 2, 2)), dma((5, 2, 2, 2)),
            dma((3, 2)),
            dma((3, 2)), dma((2, 2)),
        ],
        compiler_params=pltpu.CompilerParams(
            collective_id=0, has_side_effects=True, vmem_limit_bytes=60 * 1024 * 1024
        ),
    )(
        layer_input.T, q_latent, w_dkv, kv_gain.reshape(1, LAT), w_uq, w_uk, w_uv, w_o,
        block_order, block_order.reshape(1, 32), owner_slot.reshape(1, 32),
    )

    def hand_over(block, owned, out_ref, own_ref):
        core = lax.axis_index("tp") % 2
        block = block[...]
        out_ref[...] = jnp.where(core == 0, block[:, :448], block[:, 448:]).T
        own_ref[...] = owned[...]

    out, own = pl.pallas_call(
        hand_over,
        out_shape=(
            jax.ShapeDtypeStruct((448, ROWS), BF16),
            jax.ShapeDtypeStruct((KVW, ROWS), BF16),
        ),
        in_specs=[vmem, vmem],
        out_specs=(vmem, vmem),
    )(out, own)
    return out.T, own.T


def solution(mesh):
    return jax.shard_map(
        per_device,
        mesh=mesh,
        in_specs=(
            P("ctx", "tp"),
            P("ctx", None),
            P("tp", None),
            P(),
            P(None, "tp"),
            P("tp", None, None),
            P("tp", None, None),
            P("tp", None),
            P(),
            P(),
        ),
        out_specs=(P("ctx", "tp"), P("ctx", None)),
        check_vma=False,
    )
```
